32 devices in a mesh: row: 8 (over y, x, core), col: 4 (over z).
Axes of the slice: x: 2, y: 2, z: 4, core: 2. Of those that a mesh axis runs over, the one named last changes fastest.
Arguments:
- slip_rate: bfloat16 [32, 8, 128, 256], P('row', 'col'), may hold values from -6 to 6
- near_lists: int32 [32, 8, 6], P('row', 'col'), may hold values from 0 to 8, as said below
- near_blocks: bfloat16 [32, 8, 6, 128, 128], P('row', 'col'), may hold values from -0.21875 to 0.21875
- source_basis: bfloat16 [32, 8, 64, 128], P('row', 'col'), may hold values from -0.5 to 0.5
- target_basis: bfloat16 [32, 8, 64, 128], P('row', 'col'), may hold values from -0.75 to 0.75
- leaf_up: float32 [32, 8, 64, 64], P('row', 'col'), may hold values from -0.25 to 0.25
- leaf_down: float32 [32, 8, 64, 64], P('row', 'col'), may hold values from -0.75 to 0.75
- strip_up: float32 [8, 2, 2, 64, 64], P('row'), may hold values from -0.5 to 0.5
- strip_down: float32 [8, 2, 2, 64, 64], P('row'), may hold values from -0.75 to 0.75
- strip_lists: int32 [8, 4], P('row'), may hold values from 0 to 7, as said below
- coupling: float32 [8, 4, 64, 64], P('row'), may hold values from -0.375 to 0.375
Outputs:
- stress_rate: bfloat16 [32, 8, 128, 256], P('row', 'col')
The draws below stay inside these ranges and needn't reach their ends.
Inputs may be any that keep to these rules, and one draw needn't show every extreme that they name: `near_lists`: entry q names the neighbour leaf at offset (q // 3 - 1, q % 3 - 1); the first entry of every leaf is 4, its own block; the 6 entries of one leaf are distinct. `strip_lists`: strip r lists 4 distinct strips s with |s - r| >= 2.
All inputs are finite; a program needn't handle non-finite values.
Results may differ from the reference program's by a relative error of at most 0.0047.
Values may be sent and summed in bfloat16 or wider, within the bound.
A program may use at most 64 MiB of HBM per device.

```python
import jax
import jax.numpy as jnp
from jax import lax

LEAF = 128
RANK = 64
MEMBERS = 256
NEAR = 6
ALONG = 4
DIP = 2
CLEV = 2
FAR_STRIPS = 4
STRIKE_LEAVES = 32
DIP_LEAVES = 8
N_ROW = 8
N_COL = 4


def draw_near_lists(key, part):
    key = jax.random.fold_in(key, 5)
    slot_index = jnp.arange(8, dtype=jnp.int32)[None, None, :]
    ranking = jax.random.randint(key, (STRIKE_LEAVES, DIP_LEAVES, 8), 0, 1048576, dtype=jnp.int32) * 8 + slot_index
    picked = lax.top_k(ranking, NEAR - 1)[1].astype(jnp.int32)
    others = picked + (picked >= 4).astype(jnp.int32)
    own_block = jnp.full((STRIKE_LEAVES, DIP_LEAVES, 1), 4, dtype=jnp.int32)
    return jnp.concatenate([own_block, others], axis=2)


def draw_strip_lists(key, part):
    key = jax.random.fold_in(key, 11)
    target_strip = jnp.arange(N_ROW, dtype=jnp.int32)[:, None]
    source_strip = jnp.arange(N_ROW, dtype=jnp.int32)[None, :]
    ranking = jax.random.randint(key, (N_ROW, N_ROW), 0, 1048576, dtype=jnp.int32) * N_ROW + source_strip
    corner_pair = (target_strip == 0) & (source_strip == N_ROW - 1) | (target_strip == N_ROW - 1) & (source_strip == 0)
    ranking = jnp.where(corner_pair, ranking + 67108864, ranking)
    ranking = jnp.where(jnp.abs(target_strip - source_strip) <= 1, -1 - source_strip, ranking)
    return lax.top_k(ranking, FAR_STRIPS)[1].astype(jnp.int32)


def level_of(rng, shape, cuts, least, largest):
    level, own = 1.0, jax.random.fold_in(rng, 6)
    for axis_at, blocks in cuts:
        heights = jnp.exp(jax.random.uniform(jax.random.fold_in(own, axis_at), (blocks,), jnp.float32, least / len(cuts), largest / len(cuts)))
        level = level * jnp.repeat(heights, shape[axis_at] // blocks).reshape([-1 if axis == axis_at else 1 for axis in range(len(shape))])
    return level


def bell_draw(stream_key, dims, width, reach, split=(), kind=jnp.bfloat16):
    drawn = width * jax.random.normal(stream_key, dims, jnp.float32)
    if split:
        drawn = drawn * level_of(stream_key, dims, split, -0.22, 0.18)
    return jnp.clip(drawn, -reach, reach).astype(kind)


def setup_inputs(seed: int = 0) -> dict:
    key_of = jax.random.split(jax.random.key(seed), 12)
    slip_rate = bell_draw(key_of[0], (STRIKE_LEAVES, DIP_LEAVES, LEAF, MEMBERS), 1.0, 6.0, ((0, 8), (1, 4)))
    near_lists = draw_near_lists(jax.random.fold_in(key_of[11], 71), 0)
    near_blocks = bell_draw(key_of[2], (STRIKE_LEAVES, DIP_LEAVES, NEAR, LEAF, LEAF), (LEAF * NEAR) ** -0.5, 0.21875, ((0, 8), (1, 4)))
    source_basis = bell_draw(key_of[3], (STRIKE_LEAVES, DIP_LEAVES, RANK, LEAF), LEAF ** -0.5, 0.5, ((0, 8), (1, 4)))
    target_basis = bell_draw(key_of[4], (STRIKE_LEAVES, DIP_LEAVES, RANK, LEAF), RANK ** -0.5, 0.75, ((0, 8), (1, 4)))
    leaf_up = bell_draw(key_of[5], (STRIKE_LEAVES, DIP_LEAVES, RANK, RANK), (RANK * ALONG * DIP) ** -0.5, 0.25, ((0, 8), (1, 4)), jnp.float32)
    leaf_down = bell_draw(key_of[6], (STRIKE_LEAVES, DIP_LEAVES, RANK, RANK), RANK ** -0.5, 0.75, ((0, 8), (1, 4)), jnp.float32)
    strip_up = bell_draw(key_of[7], (N_ROW, CLEV, 2, RANK, RANK), (2 * RANK) ** -0.5, 0.5, ((0, 8),), jnp.float32)
    strip_down = bell_draw(key_of[8], (N_ROW, CLEV, 2, RANK, RANK), RANK ** -0.5, 0.75, ((0, 8),), jnp.float32)
    strip_lists = draw_strip_lists(jax.random.fold_in(key_of[11], 71), 0)
    coupling = bell_draw(key_of[10], (N_ROW, FAR_STRIPS, RANK, RANK), (RANK * FAR_STRIPS) ** -0.5, 0.375, ((0, 8),), jnp.float32)
    return dict(slip_rate=slip_rate, near_lists=near_lists, near_blocks=near_blocks, source_basis=source_basis, target_basis=target_basis, leaf_up=leaf_up, leaf_down=leaf_down, strip_up=strip_up, strip_down=strip_down, strip_lists=strip_lists, coupling=coupling)


def reference(slip_rate, near_lists, near_blocks, source_basis, target_basis, leaf_up, leaf_down, strip_up, strip_down, strip_lists, coupling):
    highest = lax.Precision.HIGHEST
    strike_count = slip_rate.shape[0]
    dip_count = slip_rate.shape[1]
    rank_width = source_basis.shape[2]
    member_count = slip_rate.shape[3]
    padded = jnp.pad(slip_rate, ((1, 1), (1, 1), (0, 0), (0, 0)))

    def near_row(strip_row):
        rows = lax.dynamic_slice_in_dim(padded, strip_row.astype(jnp.int32), 3, 0)
        views = jnp.stack([rows[row_off, col_off:col_off + dip_count] for row_off in range(3) for col_off in range(3)], axis=1)
        leaf_lists = lax.dynamic_index_in_dim(near_lists, strip_row.astype(jnp.int32), 0, keepdims=False)
        chosen = jnp.take_along_axis(views, leaf_lists[:, :, None, None], axis=1)
        blocks = lax.dynamic_index_in_dim(near_blocks, strip_row.astype(jnp.int32), 0, keepdims=False)
        return jnp.einsum("bnij,bnje->bie", blocks.astype(jnp.float32), chosen.astype(jnp.float32), precision=highest)

    near_field = lax.map(near_row, jnp.arange(strike_count, dtype=jnp.int32))

    moments = jnp.einsum("abkt,abte->abke", source_basis.astype(jnp.float32), slip_rate.astype(jnp.float32), precision=highest)
    carried = jnp.einsum("abkq,abqe->abke", leaf_up, moments, precision=highest)
    carried = carried.reshape(N_ROW, ALONG, N_COL, DIP, rank_width, member_count)
    node_moments = jnp.sum(carried, axis=(1, 3))
    for tree_level in range(CLEV):
        left_half = node_moments[:, 0::2]
        right_half = node_moments[:, 1::2]
        node_moments = jnp.einsum("rkq,rjqe->rjke", strip_up[:, tree_level, 0], left_half, precision=highest) + jnp.einsum("rkq,rjqe->rjke", strip_up[:, tree_level, 1], right_half, precision=highest)
    top_moments = node_moments[:, 0]

    strip_coeff = jnp.einsum("rakq,raqe->rke", coupling, top_moments[strip_lists], precision=highest)

    node_coeff = strip_coeff[:, None]
    for tree_level in reversed(range(CLEV)):
        first_child = jnp.einsum("rkq,rjqe->rjke", strip_down[:, tree_level, 0], node_coeff, precision=highest)
        second_child = jnp.einsum("rkq,rjqe->rjke", strip_down[:, tree_level, 1], node_coeff, precision=highest)
        node_coeff = jnp.stack([first_child, second_child], axis=2).reshape(N_ROW, -1, rank_width, member_count)
    spread = jnp.broadcast_to(node_coeff[:, None, :, None], (N_ROW, ALONG, N_COL, DIP, rank_width, member_count))
    spread = spread.reshape(strike_count, dip_count, rank_width, member_count)
    leaf_coeff = jnp.einsum("abkq,abqe->abke", leaf_down, spread, precision=highest).astype(jnp.bfloat16)
    far_field = jnp.einsum("abkt,abke->abte", target_basis.astype(jnp.float32), leaf_coeff.astype(jnp.float32), precision=highest)
    return (near_field + far_field).astype(jnp.bfloat16)
```

```python
import functools

import jax
import jax.numpy as jnp
from jax import lax
from jax.experimental import pallas as pl
from jax.experimental.pallas import tpu as pltpu
from jax.sharding import PartitionSpec as P

F32, BF16 = jnp.float32, jnp.bfloat16
MESH = pl.DeviceIdType.MESH


def dot(a, b):
    return jnp.dot(a, b, preferred_element_type=F32)


def split(x):
    high = x.astype(BF16)
    return high, (x - high.astype(F32)).astype(BF16)


def dot3(a, b):
    a_high, a_low = split(a)
    b_high, b_low = split(b)
    return dot(a_high, b_high) + (dot(a_high, b_low) + dot(a_low, b_high))


def kernel(
    n_row,
    n_col,
    lists,
    strips,
    slip_hbm,
    near_hbm,
    source_hbm,
    target_hbm,
    up_hbm,
    down_hbm,
    strip_up_hbm,
    strip_down_hbm,
    coupling_hbm,
    out,
    pad,
    near,
    source,
    target,
    up,
    down,
    strip_up,
    strip_down,
    coupling,
    acc,
    part_send,
    part_recv,
    tops,
    coeff,
    lift_high,
    lift_low,
    pair_high,
    pair_low,
    load_sem,
    halo_send,
    halo_recv,
    part_sems,
    part_rsems,
    top_sems,
    top_rsems,
    coeff_sems,
):
    along, dip = slip_hbm.shape[:2]
    rank = source.shape[2]
    levels = strip_up.shape[1]
    n_far = coupling.shape[1]
    n_near = lists.shape[2]
    half = part_send.shape[2]
    row, col = lax.axis_index("row"), lax.axis_index("col")

    barrier = pltpu.get_barrier_semaphore()
    for j in range(1, n_row):
        pl.semaphore_signal(barrier, inc=1, device_id={"row": lax.rem(row + j, n_row)}, device_id_type=MESH)
    for j in range(1, n_col):
        pl.semaphore_signal(barrier, inc=1, device_id={"col": lax.rem(col + j, n_col)}, device_id_type=MESH)

    loads = [
        pltpu.make_async_copy(src, dst, load_sem.at[k])
        for k, (src, dst) in enumerate(
            [
                (slip_hbm, pad.at[pl.ds(1, along), pl.ds(1, dip)]),
                (source_hbm, source),
                (up_hbm, up),
                (strip_up_hbm, strip_up),
                (near_hbm, near.at[:, :, pl.ds(0, n_near)]),
                (coupling_hbm, coupling),
                (strip_down_hbm, strip_down),
                (down_hbm, down),
                (target_hbm, target),
            ]
        )
    ]
    for load in loads:
        load.start()

    has = {"W": col > 0, "E": col < n_col - 1, "N": row > 0, "S": row < n_row - 1}
    there = {"W": {"col": col - 1}, "E": {"col": col + 1}, "N": {"row": row - 1}, "S": {"row": row + 1}}
    back = {"W": "E", "E": "W", "N": "S", "S": "N"}
    slot_of = {}

    def halo(name, side, src, dst):
        k = slot_of.setdefault(name, len(slot_of))
        return pltpu.make_async_remote_copy(
            src_ref=src, dst_ref=dst, send_sem=halo_send.at[k], recv_sem=halo_recv.at[k],
            device_id=there[side], device_id_type=MESH,
        )

    def rim(side, g, n):
        src = slip_hbm.at[pl.ds(g, n), pl.ds(0 if side == "W" else dip - 1, 1)]
        dst = pad.at[pl.ds(1 + g, n), pl.ds(dip + 1 if side == "W" else 0, 1)]
        return halo((side, g), side, src, dst)

    def strike(side):
        src = slip_hbm.at[pl.ds(0 if side == "N" else along - 1, 1)]
        dst = pad.at[pl.ds(along + 1 if side == "N" else 0, 1), pl.ds(1, dip)]
        return halo((side, "own"), side, src, dst)

    def corner(side, edge):
        at = 0 if edge == "W" else dip + 1
        src = pad.at[pl.ds(1 if side == "N" else along, 1), pl.ds(at, 1)]
        dst = pad.at[pl.ds(along + 1 if side == "N" else 0, 1), pl.ds(at, 1)]
        return halo((side, edge), side, src, dst)

    first_rim = [(0, 1), (along - 1, 1)]
    later_rim = [(1, along - 2)]

    pl.semaphore_wait(barrier, n_row + n_col - 2)

    for g, n in first_rim:
        for side in "WE":
            pl.when(has[side])(lambda: rim(side, g, n).start())
    for side in "NS":
        pl.when(has[side])(lambda: strike(side).start())

    empty = jnp.zeros((along + 2, 1) + pad.shape[2:], pad.dtype)
    for side, at in (("W", 0), ("E", dip + 1)):
        @pl.when(jnp.logical_not(has[side]))
        def _():
            pad[:, pl.ds(at, 1)] = empty
    for side, at in (("N", 0), ("S", along + 1)):
        @pl.when(jnp.logical_not(has[side]))
        def _():
            pad[pl.ds(at, 1)] = jnp.zeros((1,) + pad.shape[1:], pad.dtype)
    near[:, :, n_near] = jnp.zeros((along, dip) + near.shape[3:], near.dtype)

    leaves = [(g, h) for g in range(along) for h in range(dip)]
    for load in loads[1:4]:
        load.wait()
    lift = strip_up[0, 0, lax.rem(col, 2)]
    for level in range(1, levels):
        lift = dot3(strip_up[0, level, lax.rem(col // 2**level, 2)], lift)
    gather_up = jnp.concatenate([up[g, h] for g, h in leaves], axis=1)
    loads[0].wait()
    moments = jnp.concatenate([dot(source[g, h], pad[g + 1, h + 1]) for g, h in leaves], axis=0)
    lifted = dot3(lift, dot3(gather_up, moments))

    def part(j):
        to = lax.rem(col + j, n_col)
        return pltpu.make_async_remote_copy(
            src_ref=part_send.at[lax.rem(to, 2)], dst_ref=part_recv.at[j],
            send_sem=part_sems.at[j], recv_sem=part_rsems.at[j],
            device_id={"col": to}, device_id_type=MESH,
        )

    for k in range(2):
        part_send[k] = lifted[:, k * half : (k + 1) * half].astype(part_send.dtype)
    for j in range(1, n_col):
        part(j).start()
    for g, n in later_rim:
        for side in "WE":
            pl.when(has[side])(lambda: rim(side, g, n).start())

    loads[4].wait()

    def place(g, h, q):
        index = n_near
        for n in range(n_near):
            index = jnp.where(lists[g, h, n] == q, n, index)
        return index

    def wave(g, h, wanted):
        found = [
            (q, g + q // 3, h + q % 3)
            for q in range(9)
            if wanted == (1 <= g + q // 3 <= along, 1 <= h + q % 3 <= dip)
        ]
        if not found:
            return None
        blocks = jnp.concatenate([near[g, h, place(g, h, q)] for q, _, _ in found], axis=1)
        fields = jnp.concatenate([pad[a, b] for _, a, b in found], axis=0)
        return dot(blocks, fields)

    for g, h in leaves:
        acc[g, h] = wave(g, h, (True, True))

    for g, n in first_rim:
        for side in "WE":
            pl.when(has[back[side]])(lambda: rim(side, g, n).wait_recv())
    for edge in "WE":
        for side in "NS":
            pl.when(jnp.logical_and(has[side], has[edge]))(lambda: corner(side, edge).start())

    for j in range(1, n_col):
        part(j).wait_recv()
    mine = lax.rem(col, 2)
    total = part_send[mine].astype(F32)
    for j in range(1, n_col):
        total = total + part_recv[j].astype(F32)
    tops[row] = total.astype(tops.dtype)

    def top(j, owner):
        return pltpu.make_async_remote_copy(
            src_ref=tops.at[owner], dst_ref=tops.at[owner],
            send_sem=top_sems.at[j], recv_sem=top_rsems.at[j],
            device_id={"row": lax.rem(row + j, n_row)}, device_id_type=MESH,
        )

    for j in range(1, n_row):
        top(j, row).start()

    for load in loads[5:]:
        load.wait()
    lower = strip_down[0, levels - 1, lax.rem(col // 2 ** (levels - 1), 2)]
    for level in reversed(range(levels - 1)):
        lower = dot3(strip_down[0, level, lax.rem(col // 2**level, 2)], lower)
    lift_high[...], lift_low[...] = split(dot3(down[...].reshape(along * dip * rank, rank), lower))
    pair_high[...], pair_low[...] = split(jnp.concatenate([coupling[0, a] for a in range(n_far)], axis=1))

    for j in range(1, n_row):
        top(j, lax.rem(row + n_row - j, n_row)).wait_recv()
    chosen = jnp.concatenate([tops[strips[0, a]] for a in range(n_far)], axis=0)
    coeff[mine] = dot(pair_high[...], chosen) + dot(pair_low[...], chosen)
    swap = pltpu.make_async_remote_copy(
        src_ref=coeff.at[mine], dst_ref=coeff.at[mine],
        send_sem=coeff_sems.at[0], recv_sem=coeff_sems.at[1],
        device_id={"col": col + 1 - 2 * mine}, device_id_type=MESH,
    )
    swap.start()

    for g, n in later_rim:
        for side in "WE":
            pl.when(has[back[side]])(lambda: rim(side, g, n).wait_recv())
    for g, h in leaves:
        acc[g, h] += wave(g, h, (True, False))
    for side in "NS":
        pl.when(has[back[side]])(lambda: strike(side).wait_recv())
    for g, h in leaves:
        if g in (0, along - 1):
            acc[g, h] += wave(g, h, (False, True))
    for edge in "WE":
        for side in "NS":
            pl.when(jnp.logical_and(has[back[side]], has[edge]))(lambda: corner(side, edge).wait_recv())
    for g, h in leaves:
        if g in (0, along - 1):
            acc[g, h] += wave(g, h, (False, False))

    other = coeff.at[1 - mine]
    pltpu.make_async_remote_copy(
        src_ref=other, dst_ref=other, send_sem=coeff_sems.at[0], recv_sem=coeff_sems.at[1],
        device_id={"col": col + 1 - 2 * mine}, device_id_type=MESH,
    ).wait_recv()
    c_high, c_low = split(jnp.concatenate([coeff[0], coeff[1]], axis=1))
    for k, (g, h) in enumerate(leaves):
        rows = pl.ds(k * rank, rank)
        e_high = lift_high[rows]
        leaf = (dot(e_high, c_high) + (dot(e_high, c_low) + dot(lift_low[rows], c_high))).astype(BF16)
        far = lax.dot_general(target[g, h], leaf, (((0,), (0,)), ((), ())), preferred_element_type=F32)
        out[g, h] = (acc[g, h] + far).astype(out.dtype)

    for g, n in first_rim + later_rim:
        for side in "WE":
            pl.when(has[side])(lambda: rim(side, g, n).wait_send())
    for side in "NS":
        pl.when(has[side])(lambda: strike(side).wait_send())
        for edge in "WE":
            pl.when(jnp.logical_and(has[side], has[edge]))(lambda: corner(side, edge).wait_send())
    for j in range(1, n_col):
        part(j).wait_send()
    for j in range(1, n_row):
        top(j, row).wait_send()
    swap.wait_send()


def body(
    n_row,
    n_col,
    slip_rate,
    near_lists,
    near_blocks,
    source_basis,
    target_basis,
    leaf_up,
    leaf_down,
    strip_up,
    strip_down,
    strip_lists,
    coupling,
):
    along, dip, leaf, members = slip_rate.shape
    rank = source_basis.shape[2]
    n_near = near_lists.shape[2]
    n_far = coupling.shape[1]
    half = members // 2
    whole = pl.BlockSpec(memory_space=pl.ANY)
    dma = pltpu.SemaphoreType.DMA
    return pl.pallas_call(
        functools.partial(kernel, n_row, n_col),
        out_shape=jax.ShapeDtypeStruct(slip_rate.shape, BF16),
        in_specs=[pl.BlockSpec(memory_space=pltpu.SMEM)] * 2 + [whole] * 9,
        out_specs=pl.BlockSpec(memory_space=pltpu.VMEM),
        scratch_shapes=[
            pltpu.VMEM((along + 2, dip + 2, leaf, members), BF16),
            pltpu.VMEM((along, dip, n_near + 1, leaf, leaf), BF16),
            pltpu.VMEM(source_basis.shape, BF16),
            pltpu.VMEM(target_basis.shape, BF16),
            pltpu.VMEM(leaf_up.shape, F32),
            pltpu.VMEM(leaf_down.shape, F32),
            pltpu.VMEM(strip_up.shape, F32),
            pltpu.VMEM(strip_down.shape, F32),
            pltpu.VMEM(coupling.shape, F32),
            pltpu.VMEM(slip_rate.shape, F32),
            pltpu.VMEM((2, rank, half), BF16),
            pltpu.VMEM((n_col, rank, half), BF16),
            pltpu.VMEM((n_row, rank, half), BF16),
            pltpu.VMEM((2, rank, half), F32),
            pltpu.VMEM((along * dip * rank, rank), BF16),
            pltpu.VMEM((along * dip * rank, rank), BF16),
            pltpu.VMEM((rank, n_far * rank), BF16),
            pltpu.VMEM((rank, n_far * rank), BF16),
            dma((9,)),
            dma((12,)),
            dma((12,)),
            dma((n_col,)),
            dma((n_col,)),
            dma((n_row,)),
            dma((n_row,)),
            dma((2,)),
        ],
        compiler_params=pltpu.CompilerParams(
            collective_id=0, has_side_effects=True, vmem_limit_bytes=40 * 1024 * 1024
        ),
    )(
        near_lists,
        strip_lists,
        slip_rate,
        near_blocks,
        source_basis,
        target_basis,
        leaf_up,
        leaf_down,
        strip_up,
        strip_down,
        coupling,
    )


def solution(mesh):
    in_specs = (
        P("row", "col", None, None),
        P("row", "col", None),
        P("row", "col", None, None, None),
        P("row", "col", None, None),
        P("row", "col", None, None),
        P("row", "col", None, None),
        P("row", "col", None, None),
        P("row", None, None, None, None),
        P("row", None, None, None, None),
        P("row", None),
        P("row", None, None, None),
    )
    out_specs = P("row", "col", None, None)
    run = functools.partial(body, mesh.shape["row"], mesh.shape["col"])
    return jax.shard_map(run, mesh=mesh, in_specs=in_specs, out_specs=out_specs, check_vma=False)
```

```python
import functools

import jax
import jax.numpy as jnp
from jax import lax
from jax.experimental import pallas as pl
from jax.experimental.pallas import tpu as pltpu
from jax.sharding import PartitionSpec as P

F32, BF16 = jnp.float32, jnp.bfloat16
MESH = pl.DeviceIdType.MESH


def dot(a, b):
    return jnp.dot(a, b, preferred_element_type=F32)


def split(x):
    high = x.astype(BF16)
    return high, (x - high.astype(F32)).astype(BF16)


def dot3(a, b):
    a_high, a_low = split(a)
    b_high, b_low = split(b)
    return dot(a_high, b_high) + (dot(a_high, b_low) + dot(a_low, b_high))


def kernel(
    n_row,
    n_col,
    lists_hbm,
    strips_hbm,
    slip_hbm,
    near_hbm,
    source_hbm,
    target_hbm,
    up_hbm,
    down_hbm,
    strip_up_hbm,
    strip_down_hbm,
    coupling_hbm,
    out_hbm,
    lists,
    strips,
    out,
    pad,
    near,
    source,
    target,
    up,
    down,
    strip_up,
    strip_down,
    coupling,
    acc,
    part_send,
    part_recv,
    tops,
    coeff,
    fall,
    spread,
    pair_high,
    pair_low,
    load_sem,
    halo_send,
    halo_recv,
    part_sems,
    part_rsems,
    top_sems,
    top_rsems,
    coeff_sems,
    out_sems,
):
    along, dip = slip_hbm.shape[:2]
    rank = source.shape[2]
    levels = strip_up.shape[1]
    n_far = coupling.shape[1]
    n_near = lists.shape[2]
    half = part_send.shape[2]
    row, col = lax.axis_index("row"), lax.axis_index("col")

    barrier = pltpu.get_barrier_semaphore()
    for j in range(1, n_row):
        pl.semaphore_signal(barrier, inc=1, device_id={"row": lax.rem(row + j, n_row)}, device_id_type=MESH)
    for j in range(1, n_col):
        pl.semaphore_signal(barrier, inc=1, device_id={"col": lax.rem(col + j, n_col)}, device_id_type=MESH)

    loads = [
        pltpu.make_async_copy(src, dst, load_sem.at[k])
        for k, (src, dst) in enumerate(
            [
                (strip_up_hbm, strip_up),
                (up_hbm, up),
                (source_hbm, source),
                (slip_hbm, pad.at[pl.ds(1, along), pl.ds(1, dip)]),
                (lists_hbm, lists),
                (strips_hbm, strips),
                (near_hbm, near.at[:, :, pl.ds(0, n_near)]),
                (coupling_hbm, coupling),
                (strip_down_hbm, strip_down),
                (down_hbm, down),
                (target_hbm, target),
            ]
        )
    ]
    for load in loads:
        load.start()

    has = {"W": col > 0, "E": col < n_col - 1, "N": row > 0, "S": row < n_row - 1}
    there = {"W": {"col": col - 1}, "E": {"col": col + 1}, "N": {"row": row - 1}, "S": {"row": row + 1}}
    back = {"W": "E", "E": "W", "N": "S", "S": "N"}
    slot_of = {}

    def halo(name, side, src, dst):
        k = slot_of.setdefault(name, len(slot_of))
        return pltpu.make_async_remote_copy(
            src_ref=src, dst_ref=dst, send_sem=halo_send.at[k], recv_sem=halo_recv.at[k],
            device_id=there[side], device_id_type=MESH,
        )

    def rim(side, g, n):
        src = slip_hbm.at[pl.ds(g, n), pl.ds(0 if side == "W" else dip - 1, 1)]
        dst = pad.at[pl.ds(1 + g, n), pl.ds(dip + 1 if side == "W" else 0, 1)]
        return halo((side, g), side, src, dst)

    def strike(side):
        src = slip_hbm.at[pl.ds(0 if side == "N" else along - 1, 1)]
        dst = pad.at[pl.ds(along + 1 if side == "N" else 0, 1), pl.ds(1, dip)]
        return halo((side, "own"), side, src, dst)

    def corner(side, edge):
        at = 0 if edge == "W" else dip + 1
        src = pad.at[pl.ds(1 if side == "N" else along, 1), pl.ds(at, 1)]
        dst = pad.at[pl.ds(along + 1 if side == "N" else 0, 1), pl.ds(at, 1)]
        return halo((side, edge), side, src, dst)

    first_rim = [(0, 1), (along - 1, 1)]
    later_rim = [(1, along - 2)]

    leaves = [(g, h) for g in range(along) for h in range(dip)]
    loads[0].wait()
    lift = strip_up[0, 0, lax.rem(col, 2)]
    for level in range(1, levels):
        lift = dot3(strip_up[0, level, lax.rem(col // 2**level, 2)], lift)
    loads[1].wait()
    gather_up = jnp.concatenate([up[g, h] for g, h in leaves], axis=1)
    loads[2].wait()
    loads[3].wait()
    moments = jnp.concatenate([dot(source[g, h], pad[g + 1, h + 1]) for g, h in leaves], axis=0)
    lifted = dot3(lift, dot3(gather_up, moments))
    for k in range(2):
        part_send[k] = lifted[:, k * half : (k + 1) * half].astype(part_send.dtype)

    def part(j):
        to = lax.rem(col + j, n_col)
        return pltpu.make_async_remote_copy(
            src_ref=part_send.at[lax.rem(to, 2)], dst_ref=part_recv.at[j],
            send_sem=part_sems.at[j], recv_sem=part_rsems.at[j],
            device_id={"col": to}, device_id_type=MESH,
        )

    pl.semaphore_wait(barrier, n_row + n_col - 2)

    for j in range(1, n_col):
        part(j).start()
    for g, n in first_rim:
        for side in "WE":
            pl.when(has[side])(lambda: rim(side, g, n).start())
    for side in "NS":
        pl.when(has[side])(lambda: strike(side).start())
    for g, n in later_rim:
        for side in "WE":
            pl.when(has[side])(lambda: rim(side, g, n).start())

    empty = jnp.zeros((along + 2, 1) + pad.shape[2:], pad.dtype)
    for side, at in (("W", 0), ("E", dip + 1)):
        @pl.when(jnp.logical_not(has[side]))
        def _():
            pad[:, pl.ds(at, 1)] = empty
    for side, at in (("N", 0), ("S", along + 1)):
        @pl.when(jnp.logical_not(has[side]))
        def _():
            pad[pl.ds(at, 1)] = jnp.zeros((1,) + pad.shape[1:], pad.dtype)
    near[:, :, n_near] = jnp.zeros((along, dip) + near.shape[3:], near.dtype)

    for load in loads[4:7]:
        load.wait()

    def place(g, h, q):
        index = n_near
        for n in range(n_near):
            index = jnp.where(lists[g, h, n] == q, n, index)
        return index

    def wave(g, h, wanted):
        found = [
            (q, g + q // 3, h + q % 3)
            for q in range(9)
            if wanted == (1 <= g + q // 3 <= along, 1 <= h + q % 3 <= dip)
        ]
        if not found:
            return None
        blocks = jnp.concatenate([near[g, h, place(g, h, q)] for q, _, _ in found], axis=1)
        fields = jnp.concatenate([pad[a, b] for _, a, b in found], axis=0)
        return dot(blocks, fields)

    for g, h in leaves[: len(leaves) // 2]:
        acc[g, h] = wave(g, h, (True, True))

    for g, n in first_rim:
        for side in "WE":
            pl.when(has[back[side]])(lambda: rim(side, g, n).wait_recv())
    for edge in "WE":
        for side in "NS":
            pl.when(jnp.logical_and(has[side], has[edge]))(lambda: corner(side, edge).start())

    for j in range(1, n_col):
        part(j).wait_recv()
    mine = lax.rem(col, 2)
    total = part_send[mine].astype(F32)
    for j in range(1, n_col):
        total = total + part_recv[j].astype(F32)
    tops[row] = total.astype(tops.dtype)

    def top(j, owner):
        return pltpu.make_async_remote_copy(
            src_ref=tops.at[owner], dst_ref=tops.at[owner],
            send_sem=top_sems.at[j], recv_sem=top_rsems.at[j],
            device_id={"row": lax.rem(row + j, n_row)}, device_id_type=MESH,
        )

    for j in range(1, n_row):
        top(j, row).start()

    for load in loads[7:]:
        load.wait()
    pair_high[...], pair_low[...] = split(jnp.concatenate([coupling[0, a] for a in range(n_far)], axis=1))
    lower = strip_down[0, levels - 1, lax.rem(col // 2 ** (levels - 1), 2)]
    for level in reversed(range(levels - 1)):
        lower = dot3(strip_down[0, level, lax.rem(col // 2**level, 2)], lower)
    fall_high, fall_low = split(dot3(down[...].reshape(along * dip * rank, rank), lower))
    fall[...] = jnp.concatenate([fall_high, fall_low, fall_high], axis=1)
    for g, h in leaves:
        spread[g, h] = target[g, h].astype(F32).T.astype(BF16)
    for g, h in leaves[len(leaves) // 2 :]:
        acc[g, h] = wave(g, h, (True, True))

    for j in range(1, n_row):
        top(j, lax.rem(row + n_row - j, n_row)).wait_recv()
    chosen = jnp.concatenate([tops[strips[0, a]] for a in range(n_far)], axis=0)
    coeff[mine] = dot(pair_high[...], chosen) + dot(pair_low[...], chosen)

    def swap(side):
        return pltpu.make_async_remote_copy(
            src_ref=coeff.at[side], dst_ref=coeff.at[side],
            send_sem=coeff_sems.at[0], recv_sem=coeff_sems.at[1],
            device_id={"col": col + 1 - 2 * mine}, device_id_type=MESH,
        )

    swap(mine).start()

    for g, n in later_rim:
        for side in "WE":
            pl.when(has[back[side]])(lambda: rim(side, g, n).wait_recv())
    for g, h in leaves:
        acc[g, h] += wave(g, h, (True, False))
    for side in "NS":
        pl.when(has[back[side]])(lambda: strike(side).wait_recv())
    for g, h in leaves:
        if g in (0, along - 1):
            acc[g, h] += wave(g, h, (False, True))

    swap(1 - mine).wait_recv()
    c_high, c_low = split(jnp.concatenate([coeff[0], coeff[1]], axis=1))
    falls = dot(fall[...], jnp.concatenate([c_high, c_high, c_low], axis=0)).astype(BF16)

    def result(g, h):
        return pltpu.make_async_copy(out.at[g, h], out_hbm.at[g, h], out_sems.at[g, h])

    def finish(g, h, value):
        k = g * dip + h
        out[g, h] = (value + dot(spread[g, h], falls[k * rank : (k + 1) * rank])).astype(out.dtype)
        result(g, h).start()

    for g, h in leaves:
        if g not in (0, along - 1):
            finish(g, h, acc[g, h])
    for edge in "WE":
        for side in "NS":
            pl.when(jnp.logical_and(has[back[side]], has[edge]))(lambda: corner(side, edge).wait_recv())
    for g, h in leaves:
        if g in (0, along - 1):
            finish(g, h, acc[g, h] + wave(g, h, (False, False)))

    for g, n in first_rim + later_rim:
        for side in "WE":
            pl.when(has[side])(lambda: rim(side, g, n).wait_send())
    for side in "NS":
        pl.when(has[side])(lambda: strike(side).wait_send())
        for edge in "WE":
            pl.when(jnp.logical_and(has[side], has[edge]))(lambda: corner(side, edge).wait_send())
    for j in range(1, n_col):
        part(j).wait_send()
    for j in range(1, n_row):
        top(j, row).wait_send()
    swap(mine).wait_send()
    for g, h in leaves:
        result(g, h).wait()


def body(
    n_row,
    n_col,
    slip_rate,
    near_lists,
    near_blocks,
    source_basis,
    target_basis,
    leaf_up,
    leaf_down,
    strip_up,
    strip_down,
    strip_lists,
    coupling,
):
    along, dip, leaf, members = slip_rate.shape
    rank = source_basis.shape[2]
    n_near = near_lists.shape[2]
    n_far = coupling.shape[1]
    half = members // 2
    whole = pl.BlockSpec(memory_space=pltpu.HBM)
    dma = pltpu.SemaphoreType.DMA
    return pl.pallas_call(
        functools.partial(kernel, n_row, n_col),
        out_shape=jax.ShapeDtypeStruct(slip_rate.shape, BF16),
        in_specs=[whole] * 11,
        out_specs=pl.BlockSpec(memory_space=pl.ANY),
        scratch_shapes=[
            pltpu.SMEM(near_lists.shape, jnp.int32),
            pltpu.SMEM(strip_lists.shape, jnp.int32),
            pltpu.VMEM(slip_rate.shape, BF16),
            pltpu.VMEM((along + 2, dip + 2, leaf, members), BF16),
            pltpu.VMEM((along, dip, n_near + 1, leaf, leaf), BF16),
            pltpu.VMEM(source_basis.shape, BF16),
            pltpu.VMEM(target_basis.shape, BF16),
            pltpu.VMEM(leaf_up.shape, F32),
            pltpu.VMEM(leaf_down.shape, F32),
            pltpu.VMEM(strip_up.shape, F32),
            pltpu.VMEM(strip_down.shape, F32),
            pltpu.VMEM(coupling.shape, F32),
            pltpu.VMEM(slip_rate.shape, F32),
            pltpu.VMEM((2, rank, half), BF16),
            pltpu.VMEM((n_col, rank, half), BF16),
            pltpu.VMEM((n_row, rank, half), BF16),
            pltpu.VMEM((2, rank, half), F32),
            pltpu.VMEM((along * dip * rank, 3 * rank), BF16),
            pltpu.VMEM((along, dip, leaf, rank), BF16),
            pltpu.VMEM((rank, n_far * rank), BF16),
            pltpu.VMEM((rank, n_far * rank), BF16),
            dma((11,)),
            dma((12,)),
            dma((12,)),
            dma((n_col,)),
            dma((n_col,)),
            dma((n_row,)),
            dma((n_row,)),
            dma((2,)),
            dma((along, dip)),
        ],
        compiler_params=pltpu.CompilerParams(
            collective_id=0, has_side_effects=True, vmem_limit_bytes=63 * 1024 * 1024
        ),
    )(
        near_lists,
        strip_lists,
        slip_rate,
        near_blocks,
        source_basis,
        target_basis,
        leaf_up,
        leaf_down,
        strip_up,
        strip_down,
        coupling,
    )


def solution(mesh):
    in_specs = (
        P("row", "col", None, None),
        P("row", "col", None),
        P("row", "col", None, None, None),
        P("row", "col", None, None),
        P("row", "col", None, None),
        P("row", "col", None, None),
        P("row", "col", None, None),
        P("row", None, None, None, None),
        P("row", None, None, None, None),
        P("row", None),
        P("row", None, None, None),
    )
    out_specs = P("row", "col", None, None)
    run = functools.partial(body, mesh.shape["row"], mesh.shape["col"])
    return jax.shard_map(run, mesh=mesh, in_specs=in_specs, out_specs=out_specs, check_vma=False)
```

```python
import functools

import jax
import jax.numpy as jnp
from jax import lax
from jax.experimental import pallas as pl
from jax.experimental.pallas import tpu as pltpu
from jax.sharding import PartitionSpec as P

F32, BF16 = jnp.float32, jnp.bfloat16
MESH = pl.DeviceIdType.MESH


def dot(a, b):
    return jnp.dot(a, b, preferred_element_type=F32)


def split(x):
    high = x.astype(BF16)
    return high, (x - high.astype(F32)).astype(BF16)


def dot3(a, b):
    a_high, a_low = split(a)
    b_high, b_low = split(b)
    return dot(a_high, b_high) + (dot(a_high, b_low) + dot(a_low, b_high))


def kernel(
    n_row,
    n_col,
    lists_hbm,
    strips_hbm,
    slip_hbm,
    near_hbm,
    source_hbm,
    target_hbm,
    up_hbm,
    down_hbm,
    strip_up_hbm,
    strip_down_hbm,
    coupling_hbm,
    out_hbm,
    lists,
    strips,
    out,
    pad,
    near,
    source,
    target,
    up,
    down,
    strip_up,
    strip_down,
    coupling,
    acc,
    part_send,
    part_recv,
    tops,
    coeff,
    fall,
    spread,
    pair_high,
    pair_low,
    load_sem,
    halo_send,
    halo_recv,
    part_sems,
    part_rsems,
    top_sems,
    top_rsems,
    coeff_sems,
    out_sems,
):
    along, dip = slip_hbm.shape[:2]
    rank = source.shape[2]
    levels = strip_up.shape[1]
    n_far = coupling.shape[1]
    n_near = lists.shape[2]
    half = part_send.shape[2]
    row, col = lax.axis_index("row"), lax.axis_index("col")

    barrier = pltpu.get_barrier_semaphore()
    for j in range(1, n_row):
        pl.semaphore_signal(barrier, inc=1, device_id={"row": lax.rem(row + j, n_row)}, device_id_type=MESH)
    for j in range(1, n_col):
        pl.semaphore_signal(barrier, inc=1, device_id={"col": lax.rem(col + j, n_col)}, device_id_type=MESH)

    loads = [
        pltpu.make_async_copy(src, dst, load_sem.at[k])
        for k, (src, dst) in enumerate(
            [
                (strip_up_hbm, strip_up),
                (up_hbm, up),
                (source_hbm, source),
                (slip_hbm, pad.at[pl.ds(1, along), pl.ds(1, dip)]),
                (lists_hbm, lists),
                (strips_hbm, strips),
                (near_hbm, near.at[:, :, pl.ds(0, n_near)]),
                (coupling_hbm, coupling),
                (strip_down_hbm, strip_down),
                (down_hbm, down),
                (target_hbm, target),
            ]
        )
    ]
    for load in loads:
        load.start()

    has = {"W": col > 0, "E": col < n_col - 1, "N": row > 0, "S": row < n_row - 1}
    there = {"W": {"col": col - 1}, "E": {"col": col + 1}, "N": {"row": row - 1}, "S": {"row": row + 1}}
    back = {"W": "E", "E": "W", "N": "S", "S": "N"}
    slot_of = {}

    def halo(name, side, src, dst):
        k = slot_of.setdefault(name, len(slot_of))
        return pltpu.make_async_remote_copy(
            src_ref=src, dst_ref=dst, send_sem=halo_send.at[k], recv_sem=halo_recv.at[k],
            device_id=there[side], device_id_type=MESH,
        )

    def rim(side, g, n):
        src = slip_hbm.at[pl.ds(g, n), pl.ds(0 if side == "W" else dip - 1, 1)]
        dst = pad.at[pl.ds(1 + g, n), pl.ds(dip + 1 if side == "W" else 0, 1)]
        return halo((side, g), side, src, dst)

    def strike(side):
        src = slip_hbm.at[pl.ds(0 if side == "N" else along - 1, 1)]
        dst = pad.at[pl.ds(along + 1 if side == "N" else 0, 1), pl.ds(1, dip)]
        return halo((side, "own"), side, src, dst)

    def corner(side, edge):
        at = 0 if edge == "W" else dip + 1
        src = pad.at[pl.ds(1 if side == "N" else along, 1), pl.ds(at, 1)]
        dst = pad.at[pl.ds(along + 1 if side == "N" else 0, 1), pl.ds(at, 1)]
        return halo((side, edge), side, src, dst)

    first_rim = [(0, 1), (along - 1, 1)]
    later_rim = [(1, along - 2)]

    pl.semaphore_wait(barrier, n_row + n_col - 2)

    for g, n in first_rim:
        for side in "WE":
            pl.when(has[side])(lambda: rim(side, g, n).start())
    for side in "NS":
        pl.when(has[side])(lambda: strike(side).start())

    empty = jnp.zeros((along + 2, 1) + pad.shape[2:], pad.dtype)
    for side, at in (("W", 0), ("E", dip + 1)):
        @pl.when(jnp.logical_not(has[side]))
        def _():
            pad[:, pl.ds(at, 1)] = empty
    for side, at in (("N", 0), ("S", along + 1)):
        @pl.when(jnp.logical_not(has[side]))
        def _():
            pad[pl.ds(at, 1)] = jnp.zeros((1,) + pad.shape[1:], pad.dtype)
    near[:, :, n_near] = jnp.zeros((along, dip) + near.shape[3:], near.dtype)

    leaves = [(g, h) for g in range(along) for h in range(dip)]
    loads[0].wait()
    lift = strip_up[0, 0, lax.rem(col, 2)]
    for level in range(1, levels):
        lift = dot3(strip_up[0, level, lax.rem(col // 2**level, 2)], lift)
    loads[1].wait()
    gather_up = jnp.concatenate([up[g, h] for g, h in leaves], axis=1)
    loads[2].wait()
    loads[3].wait()
    moments = jnp.concatenate([dot(source[g, h], pad[g + 1, h + 1]) for g, h in leaves], axis=0)
    lifted = dot3(lift, dot3(gather_up, moments))
    for k in range(2):
        part_send[k] = lifted[:, k * half : (k + 1) * half].astype(part_send.dtype)

    def part(j):
        to = lax.rem(col + j, n_col)
        return pltpu.make_async_remote_copy(
            src_ref=part_send.at[lax.rem(to, 2)], dst_ref=part_recv.at[j],
            send_sem=part_sems.at[j], recv_sem=part_rsems.at[j],
            device_id={"col": to}, device_id_type=MESH,
        )

    for j in range(1, n_col):
        part(j).start()
    for g, n in later_rim:
        for side in "WE":
            pl.when(has[side])(lambda: rim(side, g, n).start())

    for load in loads[7:]:
        load.wait()
    pair_high[...], pair_low[...] = split(jnp.concatenate([coupling[0, a] for a in range(n_far)], axis=1))
    lower = strip_down[0, levels - 1, lax.rem(col // 2 ** (levels - 1), 2)]
    for level in reversed(range(levels - 1)):
        lower = dot3(strip_down[0, level, lax.rem(col // 2**level, 2)], lower)
    fall_high, fall_low = split(dot3(down[...].reshape(along * dip * rank, rank), lower))
    fall[...] = jnp.concatenate([fall_high, fall_low, fall_high], axis=1)
    for g, h in leaves:
        spread[g, h] = target[g, h].astype(F32).T.astype(BF16)

    for load in loads[4:7]:
        load.wait()

    def place(g, h, q):
        index = n_near
        for n in range(n_near):
            index = jnp.where(lists[g, h, n] == q, n, index)
        return index

    def wave(g, h, wanted):
        found = [
            (q, g + q // 3, h + q % 3)
            for q in range(9)
            if wanted == (1 <= g + q // 3 <= along, 1 <= h + q % 3 <= dip)
        ]
        if not found:
            return None
        blocks = jnp.concatenate([near[g, h, place(g, h, q)] for q, _, _ in found], axis=1)
        fields = jnp.concatenate([pad[a, b] for _, a, b in found], axis=0)
        return dot(blocks, fields)

    for g, h in leaves[: len(leaves) // 2]:
        acc[g, h] = wave(g, h, (True, True))

    for g, n in first_rim:
        for side in "WE":
            pl.when(has[back[side]])(lambda: rim(side, g, n).wait_recv())
    for edge in "WE":
        for side in "NS":
            pl.when(jnp.logical_and(has[side], has[edge]))(lambda: corner(side, edge).start())

    for j in range(1, n_col):
        part(j).wait_recv()
    mine = lax.rem(col, 2)
    total = part_send[mine].astype(F32)
    for j in range(1, n_col):
        total = total + part_recv[j].astype(F32)
    tops[row] = total.astype(tops.dtype)

    def top(j, owner):
        return pltpu.make_async_remote_copy(
            src_ref=tops.at[owner], dst_ref=tops.at[owner],
            send_sem=top_sems.at[j], recv_sem=top_rsems.at[j],
            device_id={"row": lax.rem(row + j, n_row)}, device_id_type=MESH,
        )

    for j in range(1, n_row):
        top(j, row).start()

    for g, h in leaves[len(leaves) // 2 :]:
        acc[g, h] = wave(g, h, (True, True))

    for j in range(1, n_row):
        top(j, lax.rem(row + n_row - j, n_row)).wait_recv()
    chosen = jnp.concatenate([tops[strips[0, a]] for a in range(n_far)], axis=0)
    coeff[mine] = dot(pair_high[...], chosen) + dot(pair_low[...], chosen)

    def swap(side):
        return pltpu.make_async_remote_copy(
            src_ref=coeff.at[side], dst_ref=coeff.at[side],
            send_sem=coeff_sems.at[0], recv_sem=coeff_sems.at[1],
            device_id={"col": col + 1 - 2 * mine}, device_id_type=MESH,
        )

    swap(mine).start()

    for g, n in later_rim:
        for side in "WE":
            pl.when(has[back[side]])(lambda: rim(side, g, n).wait_recv())
    for g, h in leaves:
        acc[g, h] += wave(g, h, (True, False))
    for side in "NS":
        pl.when(has[back[side]])(lambda: strike(side).wait_recv())
    for g, h in leaves:
        if g in (0, along - 1):
            acc[g, h] += wave(g, h, (False, True))

    swap(1 - mine).wait_recv()
    c_high, c_low = split(jnp.concatenate([coeff[0], coeff[1]], axis=1))
    falls = dot(fall[...], jnp.concatenate([c_high, c_high, c_low], axis=0)).astype(BF16)

    def result(g, h):
        return pltpu.make_async_copy(out.at[g, h], out_hbm.at[g, h], out_sems.at[g, h])

    def finish(g, h, value):
        k = g * dip + h
        out[g, h] = (value + dot(spread[g, h], falls[k * rank : (k + 1) * rank])).astype(out.dtype)
        result(g, h).start()

    for g, h in leaves:
        if g not in (0, along - 1):
            finish(g, h, acc[g, h])
    for edge in "WE":
        for side in "NS":
            pl.when(jnp.logical_and(has[back[side]], has[edge]))(lambda: corner(side, edge).wait_recv())
    for g, h in leaves:
        if g in (0, along - 1):
            finish(g, h, acc[g, h] + wave(g, h, (False, False)))

    for g, n in first_rim + later_rim:
        for side in "WE":
            pl.when(has[side])(lambda: rim(side, g, n).wait_send())
    for side in "NS":
        pl.when(has[side])(lambda: strike(side).wait_send())
        for edge in "WE":
            pl.when(jnp.logical_and(has[side], has[edge]))(lambda: corner(side, edge).wait_send())
    for j in range(1, n_col):
        part(j).wait_send()
    for j in range(1, n_row):
        top(j, row).wait_send()
    swap(mine).wait_send()
    for g, h in leaves:
        result(g, h).wait()


def body(
    n_row,
    n_col,
    slip_rate,
    near_lists,
    near_blocks,
    source_basis,
    target_basis,
    leaf_up,
    leaf_down,
    strip_up,
    strip_down,
    strip_lists,
    coupling,
):
    along, dip, leaf, members = slip_rate.shape
    rank = source_basis.shape[2]
    n_near = near_lists.shape[2]
    n_far = coupling.shape[1]
    half = members // 2
    whole = pl.BlockSpec(memory_space=pltpu.HBM)
    dma = pltpu.SemaphoreType.DMA
    operands = [
        near_lists,
        strip_lists,
        slip_rate,
        near_blocks,
        source_basis,
        target_basis,
        leaf_up,
        leaf_down,
        strip_up,
        strip_down,
        coupling,
    ]
    pinned = [pltpu.with_memory_space_constraint(x, pltpu.HBM) for x in operands]
    return pl.pallas_call(
        functools.partial(kernel, n_row, n_col),
        out_shape=jax.ShapeDtypeStruct(slip_rate.shape, BF16),
        in_specs=[whole] * 11,
        out_specs=pl.BlockSpec(memory_space=pl.ANY),
        scratch_shapes=[
            pltpu.SMEM(near_lists.shape, jnp.int32),
            pltpu.SMEM(strip_lists.shape, jnp.int32),
            pltpu.VMEM(slip_rate.shape, BF16),
            pltpu.VMEM((along + 2, dip + 2, leaf, members), BF16),
            pltpu.VMEM((along, dip, n_near + 1, leaf, leaf), BF16),
            pltpu.VMEM(source_basis.shape, BF16),
            pltpu.VMEM(target_basis.shape, BF16),
            pltpu.VMEM(leaf_up.shape, F32),
            pltpu.VMEM(leaf_down.shape, F32),
            pltpu.VMEM(strip_up.shape, F32),
            pltpu.VMEM(strip_down.shape, F32),
            pltpu.VMEM(coupling.shape, F32),
            pltpu.VMEM(slip_rate.shape, F32),
            pltpu.VMEM((2, rank, half), BF16),
            pltpu.VMEM((n_col, rank, half), BF16),
            pltpu.VMEM((n_row, rank, half), BF16),
            pltpu.VMEM((2, rank, half), F32),
            pltpu.VMEM((along * dip * rank, 3 * rank), BF16),
            pltpu.VMEM((along, dip, leaf, rank), BF16),
            pltpu.VMEM((rank, n_far * rank), BF16),
            pltpu.VMEM((rank, n_far * rank), BF16),
            dma((11,)),
            dma((12,)),
            dma((12,)),
            dma((n_col,)),
            dma((n_col,)),
            dma((n_row,)),
            dma((n_row,)),
            dma((2,)),
            dma((along, dip)),
        ],
        compiler_params=pltpu.CompilerParams(
            collective_id=0, has_side_effects=True, vmem_limit_bytes=40 * 1024 * 1024
        ),
    )(*pinned)


def solution(mesh):
    in_specs = (
        P("row", "col", None, None),
        P("row", "col", None),
        P("row", "col", None, None, None),
        P("row", "col", None, None),
        P("row", "col", None, None),
        P("row", "col", None, None),
        P("row", "col", None, None),
        P("row", None, None, None, None),
        P("row", None, None, None, None),
        P("row", None),
        P("row", None, None, None),
    )
    out_specs = P("row", "col", None, None)
    run = functools.partial(body, mesh.shape["row"], mesh.shape["col"])
    return jax.shard_map(run, mesh=mesh, in_specs=in_specs, out_specs=out_specs, check_vma=False)
```

```python
import functools

import jax
import jax.numpy as jnp
from jax import lax
from jax.experimental import pallas as pl
from jax.experimental.pallas import tpu as pltpu
from jax.sharding import PartitionSpec as P

F32, BF16 = jnp.float32, jnp.bfloat16
MESH = pl.DeviceIdType.MESH


def dot(a, b):
    return jnp.dot(a, b, preferred_element_type=F32)


def split(x):
    high = x.astype(BF16)
    return high, (x - high.astype(F32)).astype(BF16)


def dot3(a, b):
    a_high, a_low = split(a)
    b_high, b_low = split(b)
    return dot(a_high, b_high) + (dot(a_high, b_low) + dot(a_low, b_high))


def kernel(
    n_row,
    n_col,
    lists_hbm,
    strips_hbm,
    slip_hbm,
    near_hbm,
    source_hbm,
    target_hbm,
    up_hbm,
    down_hbm,
    strip_up_hbm,
    strip_down_hbm,
    coupling_hbm,
    out_hbm,
    lists,
    strips,
    out,
    pad,
    near,
    source,
    target,
    up,
    down,
    strip_up,
    strip_down,
    coupling,
    acc,
    part_send,
    part_recv,
    tops,
    coeff,
    fall,
    spread,
    pair_high,
    pair_low,
    load_sem,
    halo_send,
    halo_recv,
    part_sems,
    part_rsems,
    top_sems,
    top_rsems,
    coeff_sems,
    out_sems,
):
    along, dip = slip_hbm.shape[:2]
    rank = source.shape[2]
    levels = strip_up.shape[1]
    n_far = coupling.shape[1]
    n_near = lists.shape[2]
    half = part_send.shape[2]
    row, col = lax.axis_index("row"), lax.axis_index("col")

    barrier = pltpu.get_barrier_semaphore()
    for j in range(1, n_row):
        pl.semaphore_signal(barrier, inc=1, device_id={"row": lax.rem(row + j, n_row)}, device_id_type=MESH)
    for j in range(1, n_col):
        pl.semaphore_signal(barrier, inc=1, device_id={"col": lax.rem(col + j, n_col)}, device_id_type=MESH)

    loads = [
        pltpu.make_async_copy(src, dst, load_sem.at[k])
        for k, (src, dst) in enumerate(
            [
                (strip_up_hbm, strip_up),
                (up_hbm, up),
                (source_hbm, source),
                (slip_hbm, pad.at[pl.ds(1, along), pl.ds(1, dip)]),
                (lists_hbm, lists),
                (strips_hbm, strips),
                (near_hbm, near.at[:, :, pl.ds(0, n_near)]),
                (coupling_hbm, coupling),
                (strip_down_hbm, strip_down),
                (down_hbm, down),
                (target_hbm, target),
            ]
        )
    ]
    for load in loads:
        load.start()

    has = {"W": col > 0, "E": col < n_col - 1, "N": row > 0, "S": row < n_row - 1}
    there = {"W": {"col": col - 1}, "E": {"col": col + 1}, "N": {"row": row - 1}, "S": {"row": row + 1}}
    back = {"W": "E", "E": "W", "N": "S", "S": "N"}
    slot_of = {}

    def halo(name, side, src, dst):
        k = slot_of.setdefault(name, len(slot_of))
        return pltpu.make_async_remote_copy(
            src_ref=src, dst_ref=dst, send_sem=halo_send.at[k], recv_sem=halo_recv.at[k],
            device_id=there[side], device_id_type=MESH,
        )

    def rim(side, g, n):
        src = slip_hbm.at[pl.ds(g, n), pl.ds(0 if side == "W" else dip - 1, 1)]
        dst = pad.at[pl.ds(1 + g, n), pl.ds(dip + 1 if side == "W" else 0, 1)]
        return halo((side, g), side, src, dst)

    def strike(side):
        src = slip_hbm.at[pl.ds(0 if side == "N" else along - 1, 1)]
        dst = pad.at[pl.ds(along + 1 if side == "N" else 0, 1), pl.ds(1, dip)]
        return halo((side, "own"), side, src, dst)

    def corner(side, edge):
        at = 0 if edge == "W" else dip + 1
        src = pad.at[pl.ds(1 if side == "N" else along, 1), pl.ds(at, 1)]
        dst = pad.at[pl.ds(along + 1 if side == "N" else 0, 1), pl.ds(at, 1)]
        return halo((side, edge), side, src, dst)

    first_rim = [(0, 1), (along - 1, 1)]
    later_rim = [(1, along - 2)]

    pl.semaphore_wait(barrier, n_row + n_col - 2)

    for g, n in first_rim:
        for side in "WE":
            pl.when(has[side])(lambda: rim(side, g, n).start())

    empty = jnp.zeros((along + 2, 1) + pad.shape[2:], pad.dtype)
    for side, at in (("W", 0), ("E", dip + 1)):
        @pl.when(jnp.logical_not(has[side]))
        def _():
            pad[:, pl.ds(at, 1)] = empty
    for side, at in (("N", 0), ("S", along + 1)):
        @pl.when(jnp.logical_not(has[side]))
        def _():
            pad[pl.ds(at, 1)] = jnp.zeros((1,) + pad.shape[1:], pad.dtype)
    near[:, :, n_near] = jnp.zeros((along, dip) + near.shape[3:], near.dtype)

    leaves = [(g, h) for g in range(along) for h in range(dip)]
    loads[0].wait()
    lift = strip_up[0, 0, lax.rem(col, 2)]
    for level in range(1, levels):
        lift = dot3(strip_up[0, level, lax.rem(col // 2**level, 2)], lift)
    loads[1].wait()
    gather_up = jnp.concatenate([up[g, h] for g, h in leaves], axis=1)
    loads[2].wait()
    loads[3].wait()
    moments = jnp.concatenate([dot(source[g, h], pad[g + 1, h + 1]) for g, h in leaves], axis=0)
    lifted = dot3(lift, dot3(gather_up, moments))
    for k in range(2):
        part_send[k] = lifted[:, k * half : (k + 1) * half].astype(part_send.dtype)

    def part(j):
        to = lax.rem(col + j, n_col)
        return pltpu.make_async_remote_copy(
            src_ref=part_send.at[lax.rem(to, 2)], dst_ref=part_recv.at[j],
            send_sem=part_sems.at[j], recv_sem=part_rsems.at[j],
            device_id={"col": to}, device_id_type=MESH,
        )

    for j in range(1, n_col):
        part(j).start()
    for side in "NS":
        pl.when(has[side])(lambda: strike(side).start())

    for load in loads[7:]:
        load.wait()
    pair_high[...], pair_low[...] = split(jnp.concatenate([coupling[0, a] for a in range(n_far)], axis=1))
    lower = strip_down[0, levels - 1, lax.rem(col // 2 ** (levels - 1), 2)]
    for level in reversed(range(levels - 1)):
        lower = dot3(strip_down[0, level, lax.rem(col // 2**level, 2)], lower)
    fall_high, fall_low = split(dot3(down[...].reshape(along * dip * rank, rank), lower))
    fall[...] = jnp.concatenate([fall_high, fall_low, fall_high], axis=1)
    for g, h in leaves:
        spread[g, h] = target[g, h].astype(F32).T.astype(BF16)

    for load in loads[4:7]:
        load.wait()

    def place(g, h, q):
        index = n_near
        for n in range(n_near):
            index = jnp.where(lists[g, h, n] == q, n, index)
        return index

    def wave(g, h, wanted):
        found = [
            (q, g + q // 3, h + q % 3)
            for q in range(9)
            if wanted == (1 <= g + q // 3 <= along, 1 <= h + q % 3 <= dip)
        ]
        if not found:
            return None
        blocks = jnp.concatenate([near[g, h, place(g, h, q)] for q, _, _ in found], axis=1)
        fields = jnp.concatenate([pad[a, b] for _, a, b in found], axis=0)
        return dot(blocks, fields)

    for g, h in leaves[: len(leaves) // 2]:
        acc[g, h] = wave(g, h, (True, True))

    for j in range(1, n_col):
        part(j).wait_recv()
    mine = lax.rem(col, 2)
    total = part_send[mine].astype(F32)
    for j in range(1, n_col):
        total = total + part_recv[j].astype(F32)
    tops[row] = total.astype(tops.dtype)

    def top(j, owner):
        return pltpu.make_async_remote_copy(
            src_ref=tops.at[owner], dst_ref=tops.at[owner],
            send_sem=top_sems.at[j], recv_sem=top_rsems.at[j],
            device_id={"row": lax.rem(row + j, n_row)}, device_id_type=MESH,
        )

    for j in range(1, n_row):
        top(j, row).start()
    for g, n in later_rim:
        for side in "WE":
            pl.when(has[side])(lambda: rim(side, g, n).start())
    for g, n in first_rim:
        for side in "WE":
            pl.when(has[back[side]])(lambda: rim(side, g, n).wait_recv())
    for edge in "WE":
        for side in "NS":
            pl.when(jnp.logical_and(has[side], has[edge]))(lambda: corner(side, edge).start())


    for g, h in leaves[len(leaves) // 2 :]:
        acc[g, h] = wave(g, h, (True, True))

    for j in range(1, n_row):
        top(j, lax.rem(row + n_row - j, n_row)).wait_recv()
    chosen = jnp.concatenate([tops[strips[0, a]] for a in range(n_far)], axis=0)
    coeff[mine] = dot(pair_high[...], chosen) + dot(pair_low[...], chosen)

    def swap(side):
        return pltpu.make_async_remote_copy(
            src_ref=coeff.at[side], dst_ref=coeff.at[side],
            send_sem=coeff_sems.at[0], recv_sem=coeff_sems.at[1],
            device_id={"col": col + 1 - 2 * mine}, device_id_type=MESH,
        )

    swap(mine).start()

    for g, n in later_rim:
        for side in "WE":
            pl.when(has[back[side]])(lambda: rim(side, g, n).wait_recv())
    for g, h in leaves:
        acc[g, h] += wave(g, h, (True, False))
    for side in "NS":
        pl.when(has[back[side]])(lambda: strike(side).wait_recv())
    for g, h in leaves:
        if g in (0, along - 1):
            acc[g, h] += wave(g, h, (False, True))

    swap(1 - mine).wait_recv()
    c_high, c_low = split(jnp.concatenate([coeff[0], coeff[1]], axis=1))
    falls = dot(fall[...], jnp.concatenate([c_high, c_high, c_low], axis=0)).astype(BF16)

    def result(g, h):
        return pltpu.make_async_copy(out.at[g, h], out_hbm.at[g, h], out_sems.at[g, h])

    def finish(g, h, value):
        k = g * dip + h
        out[g, h] = (value + dot(spread[g, h], falls[k * rank : (k + 1) * rank])).astype(out.dtype)
        result(g, h).start()

    for g, h in leaves:
        if g not in (0, along - 1):
            finish(g, h, acc[g, h])
    for edge in "WE":
        for side in "NS":
            pl.when(jnp.logical_and(has[back[side]], has[edge]))(lambda: corner(side, edge).wait_recv())
    for g, h in leaves:
        if g in (0, along - 1):
            finish(g, h, acc[g, h] + wave(g, h, (False, False)))

    for g, n in first_rim + later_rim:
        for side in "WE":
            pl.when(has[side])(lambda: rim(side, g, n).wait_send())
    for side in "NS":
        pl.when(has[side])(lambda: strike(side).wait_send())
        for edge in "WE":
            pl.when(jnp.logical_and(has[side], has[edge]))(lambda: corner(side, edge).wait_send())
    for j in range(1, n_col):
        part(j).wait_send()
    for j in range(1, n_row):
        top(j, row).wait_send()
    swap(mine).wait_send()
    for g, h in leaves:
        result(g, h).wait()


def body(
    n_row,
    n_col,
    slip_rate,
    near_lists,
    near_blocks,
    source_basis,
    target_basis,
    leaf_up,
    leaf_down,
    strip_up,
    strip_down,
    strip_lists,
    coupling,
):
    along, dip, leaf, members = slip_rate.shape
    rank = source_basis.shape[2]
    n_near = near_lists.shape[2]
    n_far = coupling.shape[1]
    half = members // 2
    whole = pl.BlockSpec(memory_space=pltpu.HBM)
    dma = pltpu.SemaphoreType.DMA
    operands = [
        near_lists,
        strip_lists,
        slip_rate,
        near_blocks,
        source_basis,
        target_basis,
        leaf_up,
        leaf_down,
        strip_up,
        strip_down,
        coupling,
    ]
    pinned = [pltpu.with_memory_space_constraint(x, pltpu.HBM) for x in operands]
    return pl.pallas_call(
        functools.partial(kernel, n_row, n_col),
        out_shape=jax.ShapeDtypeStruct(slip_rate.shape, BF16),
        in_specs=[whole] * 11,
        out_specs=pl.BlockSpec(memory_space=pl.ANY),
        scratch_shapes=[
            pltpu.SMEM(near_lists.shape, jnp.int32),
            pltpu.SMEM(strip_lists.shape, jnp.int32),
            pltpu.VMEM(slip_rate.shape, BF16),
            pltpu.VMEM((along + 2, dip + 2, leaf, members), BF16),
            pltpu.VMEM((along, dip, n_near + 1, leaf, leaf), BF16),
            pltpu.VMEM(source_basis.shape, BF16),
            pltpu.VMEM(target_basis.shape, BF16),
            pltpu.VMEM(leaf_up.shape, F32),
            pltpu.VMEM(leaf_down.shape, F32),
            pltpu.VMEM(strip_up.shape, F32),
            pltpu.VMEM(strip_down.shape, F32),
            pltpu.VMEM(coupling.shape, F32),
            pltpu.VMEM(slip_rate.shape, F32),
            pltpu.VMEM((2, rank, half), BF16),
            pltpu.VMEM((n_col, rank, half), BF16),
            pltpu.VMEM((n_row, rank, half), BF16),
            pltpu.VMEM((2, rank, half), F32),
            pltpu.VMEM((along * dip * rank, 3 * rank), BF16),
            pltpu.VMEM((along, dip, leaf, rank), BF16),
            pltpu.VMEM((rank, n_far * rank), BF16),
            pltpu.VMEM((rank, n_far * rank), BF16),
            dma((11,)),
            dma((12,)),
            dma((12,)),
            dma((n_col,)),
            dma((n_col,)),
            dma((n_row,)),
            dma((n_row,)),
            dma((2,)),
            dma((along, dip)),
        ],
        compiler_params=pltpu.CompilerParams(
            collective_id=0, has_side_effects=True, vmem_limit_bytes=40 * 1024 * 1024
        ),
    )(*pinned)


def solution(mesh):
    in_specs = (
        P("row", "col", None, None),
        P("row", "col", None),
        P("row", "col", None, None, None),
        P("row", "col", None, None),
        P("row", "col", None, None),
        P("row", "col", None, None),
        P("row", "col", None, None),
        P("row", None, None, None, None),
        P("row", None, None, None, None),
        P("row", None),
        P("row", None, None, None),
    )
    out_specs = P("row", "col", None, None)
    run = functools.partial(body, mesh.shape["row"], mesh.shape["col"])
    return jax.shard_map(run, mesh=mesh, in_specs=in_specs, out_specs=out_specs, check_vma=False)
```

```python
import functools

import jax
import jax.numpy as jnp
from jax import lax
from jax.experimental import pallas as pl
from jax.experimental.pallas import tpu as pltpu
from jax.sharding import PartitionSpec as P

F32, BF16 = jnp.float32, jnp.bfloat16
MESH = pl.DeviceIdType.MESH


def dot(a, b):
    return jnp.dot(a, b, preferred_element_type=F32)


def split(x):
    high = x.astype(BF16)
    return high, (x - high.astype(F32)).astype(BF16)


def dot3(a, b):
    a_high, a_low = split(a)
    b_high, b_low = split(b)
    return dot(a_high, b_high) + (dot(a_high, b_low) + dot(a_low, b_high))


def kernel(
    n_row,
    n_col,
    lists_hbm,
    strips_hbm,
    slip_hbm,
    near_hbm,
    source_hbm,
    target_hbm,
    up_hbm,
    down_hbm,
    strip_up_hbm,
    strip_down_hbm,
    coupling_hbm,
    out_hbm,
    lists,
    strips,
    out,
    pad,
    near,
    source,
    target,
    up,
    down,
    strip_up,
    strip_down,
    coupling,
    acc,
    part_send,
    part_recv,
    tops,
    fall,
    spread,
    pair_high,
    pair_low,
    load_sem,
    halo_send,
    halo_recv,
    part_sems,
    part_rsems,
    top_sems,
    top_rsems,
    out_sems,
):
    along, dip = slip_hbm.shape[:2]
    rank = source.shape[2]
    levels = strip_up.shape[1]
    n_far = coupling.shape[1]
    n_near = lists.shape[2]
    row, col = lax.axis_index("row"), lax.axis_index("col")

    barrier = pltpu.get_barrier_semaphore()
    for j in range(1, n_row):
        pl.semaphore_signal(barrier, inc=1, device_id={"row": lax.rem(row + j, n_row)}, device_id_type=MESH)
    for j in range(1, n_col):
        pl.semaphore_signal(barrier, inc=1, device_id={"col": lax.rem(col + j, n_col)}, device_id_type=MESH)

    loads = [
        pltpu.make_async_copy(src, dst, load_sem.at[k])
        for k, (src, dst) in enumerate(
            [
                (strip_up_hbm, strip_up),
                (up_hbm, up),
                (source_hbm, source),
                (slip_hbm, pad.at[pl.ds(1, along), pl.ds(1, dip)]),
                (lists_hbm, lists),
                (strips_hbm, strips),
                (near_hbm, near.at[:, :, pl.ds(0, n_near)]),
                (coupling_hbm, coupling),
                (strip_down_hbm, strip_down),
                (down_hbm, down),
                (target_hbm, target),
            ]
        )
    ]
    for load in loads:
        load.start()

    has = {"W": col > 0, "E": col < n_col - 1, "N": row > 0, "S": row < n_row - 1}
    there = {"W": {"col": col - 1}, "E": {"col": col + 1}, "N": {"row": row - 1}, "S": {"row": row + 1}}
    back = {"W": "E", "E": "W", "N": "S", "S": "N"}
    slot_of = {}

    def halo(name, side, src, dst):
        k = slot_of.setdefault(name, len(slot_of))
        return pltpu.make_async_remote_copy(
            src_ref=src, dst_ref=dst, send_sem=halo_send.at[k], recv_sem=halo_recv.at[k],
            device_id=there[side], device_id_type=MESH,
        )

    def rim(side, g, n):
        src = slip_hbm.at[pl.ds(g, n), pl.ds(0 if side == "W" else dip - 1, 1)]
        dst = pad.at[pl.ds(1 + g, n), pl.ds(dip + 1 if side == "W" else 0, 1)]
        return halo((side, g), side, src, dst)

    def strike(side):
        src = slip_hbm.at[pl.ds(0 if side == "N" else along - 1, 1)]
        dst = pad.at[pl.ds(along + 1 if side == "N" else 0, 1), pl.ds(1, dip)]
        return halo((side, "own"), side, src, dst)

    def corner(side, edge):
        at = 0 if edge == "W" else dip + 1
        src = pad.at[pl.ds(1 if side == "N" else along, 1), pl.ds(at, 1)]
        dst = pad.at[pl.ds(along + 1 if side == "N" else 0, 1), pl.ds(at, 1)]
        return halo((side, edge), side, src, dst)

    first_rim = [(0, 1), (along - 1, 1)]
    later_rim = [(1, along - 2)]

    pl.semaphore_wait(barrier, n_row + n_col - 2)

    for g, n in first_rim:
        for side in "WE":
            pl.when(has[side])(lambda: rim(side, g, n).start())

    empty = jnp.zeros((along + 2, 1) + pad.shape[2:], pad.dtype)
    for side, at in (("W", 0), ("E", dip + 1)):
        @pl.when(jnp.logical_not(has[side]))
        def _():
            pad[:, pl.ds(at, 1)] = empty
    for side, at in (("N", 0), ("S", along + 1)):
        @pl.when(jnp.logical_not(has[side]))
        def _():
            pad[pl.ds(at, 1)] = jnp.zeros((1,) + pad.shape[1:], pad.dtype)
    near[:, :, n_near] = jnp.zeros((along, dip) + near.shape[3:], near.dtype)

    leaves = [(g, h) for g in range(along) for h in range(dip)]
    loads[0].wait()
    lift = strip_up[0, 0, lax.rem(col, 2)]
    for level in range(1, levels):
        lift = dot3(strip_up[0, level, lax.rem(col // 2**level, 2)], lift)
    loads[1].wait()
    gather_up = jnp.concatenate([up[g, h] for g, h in leaves], axis=1)
    loads[2].wait()
    loads[3].wait()
    moments = jnp.concatenate([dot(source[g, h], pad[g + 1, h + 1]) for g, h in leaves], axis=0)
    lifted = dot3(lift, dot3(gather_up, moments))
    part_send[...] = lifted.astype(part_send.dtype)

    def part(j):
        to = lax.rem(col + j, n_col)
        return pltpu.make_async_remote_copy(
            src_ref=part_send, dst_ref=part_recv.at[j],
            send_sem=part_sems.at[j], recv_sem=part_rsems.at[j],
            device_id={"col": to}, device_id_type=MESH,
        )

    for j in range(1, n_col):
        part(j).start()
    for side in "NS":
        pl.when(has[side])(lambda: strike(side).start())

    for load in loads[7:]:
        load.wait()
    pair_high[...], pair_low[...] = split(jnp.concatenate([coupling[0, a] for a in range(n_far)], axis=1))
    lower = strip_down[0, levels - 1, lax.rem(col // 2 ** (levels - 1), 2)]
    for level in reversed(range(levels - 1)):
        lower = dot3(strip_down[0, level, lax.rem(col // 2**level, 2)], lower)
    fall_high, fall_low = split(dot3(down[...].reshape(along * dip * rank, rank), lower))
    fall[...] = jnp.concatenate([fall_high, fall_low, fall_high], axis=1)
    for g, h in leaves:
        spread[g, h] = target[g, h].astype(F32).T.astype(BF16)

    for load in loads[4:7]:
        load.wait()

    def place(g, h, q):
        index = n_near
        for n in range(n_near):
            index = jnp.where(lists[g, h, n] == q, n, index)
        return index

    def wave(g, h, wanted):
        found = [
            (q, g + q // 3, h + q % 3)
            for q in range(9)
            if wanted == (1 <= g + q // 3 <= along, 1 <= h + q % 3 <= dip)
        ]
        if not found:
            return None
        blocks = jnp.concatenate([near[g, h, place(g, h, q)] for q, _, _ in found], axis=1)
        fields = jnp.concatenate([pad[a, b] for _, a, b in found], axis=0)
        return dot(blocks, fields)

    for g, h in leaves[: len(leaves) // 2]:
        acc[g, h] = wave(g, h, (True, True))

    for j in range(1, n_col):
        part(j).wait_recv()
    total = part_send[...].astype(F32)
    for j in range(1, n_col):
        total = total + part_recv[j].astype(F32)
    tops[row] = total.astype(tops.dtype)

    def top(j, owner):
        return pltpu.make_async_remote_copy(
            src_ref=tops.at[owner], dst_ref=tops.at[owner],
            send_sem=top_sems.at[j], recv_sem=top_rsems.at[j],
            device_id={"row": lax.rem(row + j, n_row)}, device_id_type=MESH,
        )

    for j in range(1, n_row):
        top(j, row).start()
    for g, n in later_rim:
        for side in "WE":
            pl.when(has[side])(lambda: rim(side, g, n).start())
    for g, n in first_rim:
        for side in "WE":
            pl.when(has[back[side]])(lambda: rim(side, g, n).wait_recv())
    for edge in "WE":
        for side in "NS":
            pl.when(jnp.logical_and(has[side], has[edge]))(lambda: corner(side, edge).start())


    for g, h in leaves[len(leaves) // 2 :]:
        acc[g, h] = wave(g, h, (True, True))

    for j in range(1, n_row):
        top(j, lax.rem(row + n_row - j, n_row)).wait_recv()
    chosen = jnp.concatenate([tops[strips[0, a]] for a in range(n_far)], axis=0)
    c_high, c_low = split(dot(pair_high[...], chosen) + dot(pair_low[...], chosen))
    falls = dot(fall[...], jnp.concatenate([c_high, c_high, c_low], axis=0)).astype(BF16)

    for g, n in later_rim:
        for side in "WE":
            pl.when(has[back[side]])(lambda: rim(side, g, n).wait_recv())
    for g, h in leaves:
        acc[g, h] += wave(g, h, (True, False))
    for side in "NS":
        pl.when(has[back[side]])(lambda: strike(side).wait_recv())
    for g, h in leaves:
        if g in (0, along - 1):
            acc[g, h] += wave(g, h, (False, True))

    def result(g, h):
        return pltpu.make_async_copy(out.at[g, h], out_hbm.at[g, h], out_sems.at[g, h])

    def finish(g, h, value):
        k = g * dip + h
        out[g, h] = (value + dot(spread[g, h], falls[k * rank : (k + 1) * rank])).astype(out.dtype)
        result(g, h).start()

    for g, h in leaves:
        if g not in (0, along - 1):
            finish(g, h, acc[g, h])
    for g, n in first_rim + later_rim:
        for side in "WE":
            pl.when(has[side])(lambda: rim(side, g, n).wait_send())
    for side in "NS":
        pl.when(has[side])(lambda: strike(side).wait_send())
        for edge in "WE":
            pl.when(jnp.logical_and(has[side], has[edge]))(lambda: corner(side, edge).wait_send())
    for j in range(1, n_col):
        part(j).wait_send()
    for j in range(1, n_row):
        top(j, row).wait_send()
    for edge in "WE":
        for side in "NS":
            pl.when(jnp.logical_and(has[back[side]], has[edge]))(lambda: corner(side, edge).wait_recv())
    for g, h in leaves:
        if g in (0, along - 1):
            finish(g, h, acc[g, h] + wave(g, h, (False, False)))

    for g, h in leaves:
        result(g, h).wait()


def body(
    n_row,
    n_col,
    slip_rate,
    near_lists,
    near_blocks,
    source_basis,
    target_basis,
    leaf_up,
    leaf_down,
    strip_up,
    strip_down,
    strip_lists,
    coupling,
):
    along, dip, leaf, members = slip_rate.shape
    rank = source_basis.shape[2]
    n_near = near_lists.shape[2]
    n_far = coupling.shape[1]
    whole = pl.BlockSpec(memory_space=pltpu.HBM)
    dma = pltpu.SemaphoreType.DMA
    operands = [
        near_lists,
        strip_lists,
        slip_rate,
        near_blocks,
        source_basis,
        target_basis,
        leaf_up,
        leaf_down,
        strip_up,
        strip_down,
        coupling,
    ]
    pinned = [pltpu.with_memory_space_constraint(x, pltpu.HBM) for x in operands]
    return pl.pallas_call(
        functools.partial(kernel, n_row, n_col),
        out_shape=jax.ShapeDtypeStruct(slip_rate.shape, BF16),
        in_specs=[whole] * 11,
        out_specs=pl.BlockSpec(memory_space=pl.ANY),
        scratch_shapes=[
            pltpu.SMEM(near_lists.shape, jnp.int32),
            pltpu.SMEM(strip_lists.shape, jnp.int32),
            pltpu.VMEM(slip_rate.shape, BF16),
            pltpu.VMEM((along + 2, dip + 2, leaf, members), BF16),
            pltpu.VMEM((along, dip, n_near + 1, leaf, leaf), BF16),
            pltpu.VMEM(source_basis.shape, BF16),
            pltpu.VMEM(target_basis.shape, BF16),
            pltpu.VMEM(leaf_up.shape, F32),
            pltpu.VMEM(leaf_down.shape, F32),
            pltpu.VMEM(strip_up.shape, F32),
            pltpu.VMEM(strip_down.shape, F32),
            pltpu.VMEM(coupling.shape, F32),
            pltpu.VMEM(slip_rate.shape, F32),
            pltpu.VMEM((rank, members), BF16),
            pltpu.VMEM((n_col, rank, members), BF16),
            pltpu.VMEM((n_row, rank, members), BF16),
            pltpu.VMEM((along * dip * rank, 3 * rank), BF16),
            pltpu.VMEM((along, dip, leaf, rank), BF16),
            pltpu.VMEM((rank, n_far * rank), BF16),
            pltpu.VMEM((rank, n_far * rank), BF16),
            dma((11,)),
            dma((12,)),
            dma((12,)),
            dma((n_col,)),
            dma((n_col,)),
            dma((n_row,)),
            dma((n_row,)),
            dma((along, dip)),
        ],
        compiler_params=pltpu.CompilerParams(
            collective_id=0, has_side_effects=True, vmem_limit_bytes=40 * 1024 * 1024
        ),
    )(*pinned)


def solution(mesh):
    in_specs = (
        P("row", "col", None, None),
        P("row", "col", None),
        P("row", "col", None, None, None),
        P("row", "col", None, None),
        P("row", "col", None, None),
        P("row", "col", None, None),
        P("row", "col", None, None),
        P("row", None, None, None, None),
        P("row", None, None, None, None),
        P("row", None),
        P("row", None, None, None),
    )
    out_specs = P("row", "col", None, None)
    run = functools.partial(body, mesh.shape["row"], mesh.shape["col"])
    return jax.shard_map(run, mesh=mesh, in_specs=in_specs, out_specs=out_specs, check_vma=False)
```

```python
import functools

import jax
import jax.numpy as jnp
from jax import lax
from jax.experimental import pallas as pl
from jax.experimental.pallas import tpu as pltpu
from jax.sharding import PartitionSpec as P

F32, BF16 = jnp.float32, jnp.bfloat16
MESH = pl.DeviceIdType.MESH


def dot(a, b):
    return jnp.dot(a, b, preferred_element_type=F32)


def split(x):
    high = x.astype(BF16)
    return high, (x - high.astype(F32)).astype(BF16)


def dot3(a, b):
    a_high, a_low = split(a)
    b_high, b_low = split(b)
    return dot(a_high, b_high) + (dot(a_high, b_low) + dot(a_low, b_high))


def kernel(
    n_row,
    n_col,
    lists_hbm,
    strips_hbm,
    slip_hbm,
    near_hbm,
    source_hbm,
    target_hbm,
    up_hbm,
    down_hbm,
    strip_up_hbm,
    strip_down_hbm,
    coupling_hbm,
    out_hbm,
    lists,
    strips,
    out,
    pad,
    near,
    source,
    target,
    up,
    down,
    strip_up,
    strip_down,
    coupling,
    falls,
    part_send,
    part_recv,
    tops,
    fall,
    spread,
    pair_high,
    pair_low,
    load_sem,
    halo_send,
    halo_recv,
    part_sems,
    part_rsems,
    top_sems,
    top_rsems,
    out_sems,
):
    along, dip = slip_hbm.shape[:2]
    rank = source.shape[2]
    levels = strip_up.shape[1]
    n_far = coupling.shape[1]
    n_near = lists.shape[2]
    row, col = lax.axis_index("row"), lax.axis_index("col")

    barrier = pltpu.get_barrier_semaphore()
    for j in range(1, n_row):
        pl.semaphore_signal(barrier, inc=1, device_id={"row": lax.rem(row + j, n_row)}, device_id_type=MESH)
    for j in range(1, n_col):
        pl.semaphore_signal(barrier, inc=1, device_id={"col": lax.rem(col + j, n_col)}, device_id_type=MESH)

    loads = [
        pltpu.make_async_copy(src, dst, load_sem.at[k])
        for k, (src, dst) in enumerate(
            [
                (strip_up_hbm, strip_up),
                (up_hbm, up),
                (source_hbm, source),
                (slip_hbm, pad.at[pl.ds(1, along), pl.ds(1, dip)]),
                (lists_hbm, lists),
                (strips_hbm, strips),
                (near_hbm, near),
                (coupling_hbm, coupling),
                (strip_down_hbm, strip_down),
                (down_hbm, down),
                (target_hbm, target),
            ]
        )
    ]
    for load in loads:
        load.start()

    has = {"W": col > 0, "E": col < n_col - 1, "N": row > 0, "S": row < n_row - 1}
    there = {"W": {"col": col - 1}, "E": {"col": col + 1}, "N": {"row": row - 1}, "S": {"row": row + 1}}
    back = {"W": "E", "E": "W", "N": "S", "S": "N"}
    slot_of = {}

    def halo(name, side, src, dst):
        k = slot_of.setdefault(name, len(slot_of))
        return pltpu.make_async_remote_copy(
            src_ref=src, dst_ref=dst, send_sem=halo_send.at[k], recv_sem=halo_recv.at[k],
            device_id=there[side], device_id_type=MESH,
        )

    def rim(side, g, n):
        src = slip_hbm.at[pl.ds(g, n), pl.ds(0 if side == "W" else dip - 1, 1)]
        dst = pad.at[pl.ds(1 + g, n), pl.ds(dip + 1 if side == "W" else 0, 1)]
        return halo((side, g), side, src, dst)

    def strike(side):
        src = slip_hbm.at[pl.ds(0 if side == "N" else along - 1, 1)]
        dst = pad.at[pl.ds(along + 1 if side == "N" else 0, 1), pl.ds(1, dip)]
        return halo((side, "own"), side, src, dst)

    def corner(side, edge):
        at = 0 if edge == "W" else dip + 1
        src = pad.at[pl.ds(1 if side == "N" else along, 1), pl.ds(at, 1)]
        dst = pad.at[pl.ds(along + 1 if side == "N" else 0, 1), pl.ds(at, 1)]
        return halo((side, edge), side, src, dst)

    first_rim = [(0, 1), (along - 1, 1)]
    later_rim = [(1, along - 2)]

    pl.semaphore_wait(barrier, n_row + n_col - 2)

    for g, n in first_rim:
        for side in "WE":
            pl.when(has[side])(lambda: rim(side, g, n).start())

    empty = jnp.zeros((along + 2, 1) + pad.shape[2:], pad.dtype)
    for side, at in (("W", 0), ("E", dip + 1)):
        @pl.when(jnp.logical_not(has[side]))
        def _():
            pad[:, pl.ds(at, 1)] = empty
    for side, at in (("N", 0), ("S", along + 1)):
        @pl.when(jnp.logical_not(has[side]))
        def _():
            pad[pl.ds(at, 1)] = jnp.zeros((1,) + pad.shape[1:], pad.dtype)

    leaves = [(g, h) for g in range(along) for h in range(dip)]
    loads[0].wait()
    lift = strip_up[0, 0, lax.rem(col, 2)]
    for level in range(1, levels):
        lift = dot3(strip_up[0, level, lax.rem(col // 2**level, 2)], lift)
    loads[1].wait()
    gather_up = jnp.concatenate([up[g, h] for g, h in leaves], axis=1)
    loads[2].wait()
    loads[3].wait()
    moments = jnp.concatenate([dot(source[g, h], pad[g + 1, h + 1]) for g, h in leaves], axis=0)
    lifted = dot3(lift, dot3(gather_up, moments))
    part_send[...] = lifted.astype(part_send.dtype)

    def part(j):
        to = lax.rem(col + j, n_col)
        return pltpu.make_async_remote_copy(
            src_ref=part_send, dst_ref=part_recv.at[j],
            send_sem=part_sems.at[j], recv_sem=part_rsems.at[j],
            device_id={"col": to}, device_id_type=MESH,
        )

    for j in range(1, n_col):
        part(j).start()
    for side in "NS":
        pl.when(has[side])(lambda: strike(side).start())

    for load in loads[7:]:
        load.wait()
    pair_high[...], pair_low[...] = split(jnp.concatenate([coupling[0, a] for a in range(n_far)], axis=1))
    lower = strip_down[0, levels - 1, lax.rem(col // 2 ** (levels - 1), 2)]
    for level in reversed(range(levels - 1)):
        lower = dot3(strip_down[0, level, lax.rem(col // 2**level, 2)], lower)
    fall_high, fall_low = split(dot3(down[...].reshape(along * dip * rank, rank), lower))
    fall[...] = jnp.concatenate([fall_high, fall_low, fall_high], axis=1)
    for g, h in leaves:
        spread[g, h] = target[g, h].astype(F32).T.astype(BF16)

    for load in loads[4:7]:
        load.wait()


    for j in range(1, n_col):
        part(j).wait_recv()
    total = part_send[...].astype(F32)
    for j in range(1, n_col):
        total = total + part_recv[j].astype(F32)
    tops[row] = total.astype(tops.dtype)

    def top(j, owner):
        return pltpu.make_async_remote_copy(
            src_ref=tops.at[owner], dst_ref=tops.at[owner],
            send_sem=top_sems.at[j], recv_sem=top_rsems.at[j],
            device_id={"row": lax.rem(row + j, n_row)}, device_id_type=MESH,
        )

    for j in range(1, n_row):
        top(j, row).start()
    for g, n in later_rim:
        for side in "WE":
            pl.when(has[side])(lambda: rim(side, g, n).start())
    for g, n in first_rim:
        for side in "WE":
            pl.when(has[back[side]])(lambda: rim(side, g, n).wait_recv())
    for edge in "WE":
        for side in "NS":
            pl.when(jnp.logical_and(has[side], has[edge]))(lambda: corner(side, edge).start())


    for j in range(1, n_row):
        top(j, lax.rem(row + n_row - j, n_row)).wait_recv()
    chosen = jnp.concatenate([tops[strips[0, a]] for a in range(n_far)], axis=0)
    c_high, c_low = split(dot(pair_high[...], chosen) + dot(pair_low[...], chosen))
    falls[...] = dot(fall[...], jnp.concatenate([c_high, c_high, c_low], axis=0)).astype(BF16).reshape(falls.shape)

    for g, n in later_rim:
        for side in "WE":
            pl.when(has[back[side]])(lambda: rim(side, g, n).wait_recv())
    for side in "NS":
        pl.when(has[back[side]])(lambda: strike(side).wait_recv())
    def result(g, h):
        return pltpu.make_async_copy(out.at[g, h], out_hbm.at[g, h], out_sems.at[g, h])

    for g, n in first_rim + later_rim:
        for side in "WE":
            pl.when(has[side])(lambda: rim(side, g, n).wait_send())
    for side in "NS":
        pl.when(has[side])(lambda: strike(side).wait_send())
        for edge in "WE":
            pl.when(jnp.logical_and(has[side], has[edge]))(lambda: corner(side, edge).wait_send())
    for j in range(1, n_col):
        part(j).wait_send()
    for j in range(1, n_row):
        top(j, row).wait_send()
    for edge in "WE":
        for side in "NS":
            pl.when(jnp.logical_and(has[back[side]], has[edge]))(lambda: corner(side, edge).wait_recv())

    @pl.loop(0, along)
    def _(g):
        for h in range(dip):
            places = [lists[g, h, n] for n in range(n_near)]
            fields = jnp.concatenate([pad[g + q // 3, h + q % 3] for q in places], axis=0)
            blocks = jnp.concatenate([near[g, h, n] for n in range(n_near)], axis=1)
            value = dot(blocks, fields) + dot(spread[g, h], falls[g, h])
            out[g, h] = value.astype(out.dtype)
            result(g, h).start()

    for g, h in leaves:
        result(g, h).wait()


def body(
    n_row,
    n_col,
    slip_rate,
    near_lists,
    near_blocks,
    source_basis,
    target_basis,
    leaf_up,
    leaf_down,
    strip_up,
    strip_down,
    strip_lists,
    coupling,
):
    along, dip, leaf, members = slip_rate.shape
    rank = source_basis.shape[2]
    n_near = near_lists.shape[2]
    n_far = coupling.shape[1]
    whole = pl.BlockSpec(memory_space=pltpu.HBM)
    dma = pltpu.SemaphoreType.DMA
    operands = [
        near_lists,
        strip_lists,
        slip_rate,
        near_blocks,
        source_basis,
        target_basis,
        leaf_up,
        leaf_down,
        strip_up,
        strip_down,
        coupling,
    ]
    pinned = [pltpu.with_memory_space_constraint(x, pltpu.HBM) for x in operands]
    return pl.pallas_call(
        functools.partial(kernel, n_row, n_col),
        out_shape=jax.ShapeDtypeStruct(slip_rate.shape, BF16),
        in_specs=[whole] * 11,
        out_specs=pl.BlockSpec(memory_space=pl.ANY),
        scratch_shapes=[
            pltpu.SMEM(near_lists.shape, jnp.int32),
            pltpu.SMEM(strip_lists.shape, jnp.int32),
            pltpu.VMEM(slip_rate.shape, BF16),
            pltpu.VMEM((along + 2, dip + 2, leaf, members), BF16),
            pltpu.VMEM(near_blocks.shape, BF16),
            pltpu.VMEM(source_basis.shape, BF16),
            pltpu.VMEM(target_basis.shape, BF16),
            pltpu.VMEM(leaf_up.shape, F32),
            pltpu.VMEM(leaf_down.shape, F32),
            pltpu.VMEM(strip_up.shape, F32),
            pltpu.VMEM(strip_down.shape, F32),
            pltpu.VMEM(coupling.shape, F32),
            pltpu.VMEM((along, dip, rank, members), BF16),
            pltpu.VMEM((rank, members), BF16),
            pltpu.VMEM((n_col, rank, members), BF16),
            pltpu.VMEM((n_row, rank, members), BF16),
            pltpu.VMEM((along * dip * rank, 3 * rank), BF16),
            pltpu.VMEM((along, dip, leaf, rank), BF16),
            pltpu.VMEM((rank, n_far * rank), BF16),
            pltpu.VMEM((rank, n_far * rank), BF16),
            dma((11,)),
            dma((12,)),
            dma((12,)),
            dma((n_col,)),
            dma((n_col,)),
            dma((n_row,)),
            dma((n_row,)),
            dma((along, dip)),
        ],
        compiler_params=pltpu.CompilerParams(
            collective_id=0, has_side_effects=True, vmem_limit_bytes=40 * 1024 * 1024
        ),
    )(*pinned)


def solution(mesh):
    in_specs = (
        P("row", "col", None, None),
        P("row", "col", None),
        P("row", "col", None, None, None),
        P("row", "col", None, None),
        P("row", "col", None, None),
        P("row", "col", None, None),
        P("row", "col", None, None),
        P("row", None, None, None, None),
        P("row", None, None, None, None),
        P("row", None),
        P("row", None, None, None),
    )
    out_specs = P("row", "col", None, None)
    run = functools.partial(body, mesh.shape["row"], mesh.shape["col"])
    return jax.shard_map(run, mesh=mesh, in_specs=in_specs, out_specs=out_specs, check_vma=False)
```

```python
import functools

import jax
import jax.numpy as jnp
from jax import lax
from jax.experimental import pallas as pl
from jax.experimental.pallas import tpu as pltpu
from jax.sharding import PartitionSpec as P

F32, BF16 = jnp.float32, jnp.bfloat16
MESH = pl.DeviceIdType.MESH


def dot(a, b):
    return jnp.dot(a, b, preferred_element_type=F32)


def split(x):
    high = x.astype(BF16)
    return high, (x - high.astype(F32)).astype(BF16)


def dot3(a, b):
    a_high, a_low = split(a)
    b_high, b_low = split(b)
    return dot(a_high, b_high) + (dot(a_high, b_low) + dot(a_low, b_high))


def kernel(
    n_row,
    n_col,
    lists_hbm,
    strips_hbm,
    slip_hbm,
    near_hbm,
    source_hbm,
    target_hbm,
    up_hbm,
    down_hbm,
    strip_up_hbm,
    strip_down_hbm,
    coupling_hbm,
    out_hbm,
    lists,
    strips,
    out,
    pad,
    near,
    source,
    target,
    up,
    down,
    strip_up,
    strip_down,
    coupling,
    acc,
    part_send,
    part_recv,
    tops,
    fall,
    spread,
    pair_high,
    pair_low,
    load_sem,
    halo_send,
    halo_recv,
    part_sems,
    part_rsems,
    top_sems,
    top_rsems,
    out_sems,
):
    along, dip = slip_hbm.shape[:2]
    rank = source.shape[2]
    levels = strip_up.shape[1]
    n_far = coupling.shape[1]
    n_near = lists.shape[2]
    row, col = lax.axis_index("row"), lax.axis_index("col")

    barrier = pltpu.get_barrier_semaphore()
    for j in range(1, n_row):
        pl.semaphore_signal(barrier, inc=1, device_id={"row": lax.rem(row + j, n_row)}, device_id_type=MESH)
    for j in range(1, n_col):
        pl.semaphore_signal(barrier, inc=1, device_id={"col": lax.rem(col + j, n_col)}, device_id_type=MESH)

    loads = [
        pltpu.make_async_copy(src, dst, load_sem.at[k])
        for k, (src, dst) in enumerate(
            [
                (strip_up_hbm, strip_up),
                (up_hbm, up),
                (source_hbm, source),
                (slip_hbm, pad.at[pl.ds(1, along), pl.ds(1, dip)]),
                (lists_hbm, lists),
                (strips_hbm, strips),
                (near_hbm, near.at[:, :, pl.ds(0, n_near)]),
                (coupling_hbm, coupling),
                (strip_down_hbm, strip_down),
                (down_hbm, down),
                (target_hbm, target),
            ]
        )
    ]
    for load in loads:
        load.start()

    has = {"W": col > 0, "E": col < n_col - 1, "N": row > 0, "S": row < n_row - 1}
    there = {"W": {"col": col - 1}, "E": {"col": col + 1}, "N": {"row": row - 1}, "S": {"row": row + 1}}
    back = {"W": "E", "E": "W", "N": "S", "S": "N"}
    slot_of = {}

    def halo(name, side, src, dst):
        k = slot_of.setdefault(name, len(slot_of))
        return pltpu.make_async_remote_copy(
            src_ref=src, dst_ref=dst, send_sem=halo_send.at[k], recv_sem=halo_recv.at[k],
            device_id=there[side], device_id_type=MESH,
        )

    def rim(side, g, n):
        src = slip_hbm.at[pl.ds(g, n), pl.ds(0 if side == "W" else dip - 1, 1)]
        dst = pad.at[pl.ds(1 + g, n), pl.ds(dip + 1 if side == "W" else 0, 1)]
        return halo((side, g), side, src, dst)

    def strike(side):
        src = slip_hbm.at[pl.ds(0 if side == "N" else along - 1, 1)]
        dst = pad.at[pl.ds(along + 1 if side == "N" else 0, 1), pl.ds(1, dip)]
        return halo((side, "own"), side, src, dst)

    def corner(side, edge):
        at = 0 if edge == "W" else dip + 1
        src = pad.at[pl.ds(1 if side == "N" else along, 1), pl.ds(at, 1)]
        dst = pad.at[pl.ds(along + 1 if side == "N" else 0, 1), pl.ds(at, 1)]
        return halo((side, edge), side, src, dst)

    first_rim = [(0, 1), (along - 1, 1)]
    later_rim = [(1, along - 2)]

    pl.semaphore_wait(barrier, n_row + n_col - 2)

    for g, n in first_rim:
        for side in "WE":
            pl.when(has[side])(lambda: rim(side, g, n).start())
    for side in "NS":
        pl.when(has[side])(lambda: strike(side).start())

    empty = jnp.zeros((along + 2, 1) + pad.shape[2:], pad.dtype)
    for side, at in (("W", 0), ("E", dip + 1)):
        @pl.when(jnp.logical_not(has[side]))
        def _():
            pad[:, pl.ds(at, 1)] = empty
    for side, at in (("N", 0), ("S", along + 1)):
        @pl.when(jnp.logical_not(has[side]))
        def _():
            pad[pl.ds(at, 1)] = jnp.zeros((1,) + pad.shape[1:], pad.dtype)
    near[:, :, n_near] = jnp.zeros((along, dip) + near.shape[3:], near.dtype)

    leaves = [(g, h) for g in range(along) for h in range(dip)]
    loads[0].wait()
    lift = strip_up[0, 0, lax.rem(col, 2)]
    for level in range(1, levels):
        lift = dot3(strip_up[0, level, lax.rem(col // 2**level, 2)], lift)
    loads[1].wait()
    gather_up = jnp.concatenate([up[g, h] for g, h in leaves], axis=1)
    loads[2].wait()
    loads[3].wait()
    moments = jnp.concatenate([dot(source[g, h], pad[g + 1, h + 1]) for g, h in leaves], axis=0)
    lifted = dot3(lift, dot3(gather_up, moments))
    part_send[...] = lifted.astype(part_send.dtype)

    def part(j):
        to = lax.rem(col + j, n_col)
        return pltpu.make_async_remote_copy(
            src_ref=part_send, dst_ref=part_recv.at[j],
            send_sem=part_sems.at[j], recv_sem=part_rsems.at[j],
            device_id={"col": to}, device_id_type=MESH,
        )

    for j in range(1, n_col):
        part(j).start()
    for g, n in later_rim:
        for side in "WE":
            pl.when(has[side])(lambda: rim(side, g, n).start())

    for load in loads[7:]:
        load.wait()
    pair_high[...], pair_low[...] = split(jnp.concatenate([coupling[0, a] for a in range(n_far)], axis=1))
    lower = strip_down[0, levels - 1, lax.rem(col // 2 ** (levels - 1), 2)]
    for level in reversed(range(levels - 1)):
        lower = dot3(strip_down[0, level, lax.rem(col // 2**level, 2)], lower)
    fall_high, fall_low = split(dot3(down[...].reshape(along * dip * rank, rank), lower))
    fall[...] = jnp.concatenate([fall_high, fall_low, fall_high], axis=1)
    for g, h in leaves:
        spread[g, h] = target[g, h].astype(F32).T.astype(BF16)

    for load in loads[4:7]:
        load.wait()

    def place(g, h, q):
        index = n_near
        for n in range(n_near):
            index = jnp.where(lists[g, h, n] == q, n, index)
        return index

    def wave(g, h, wanted):
        found = [
            (q, g + q // 3, h + q % 3)
            for q in range(9)
            if wanted == (1 <= g + q // 3 <= along, 1 <= h + q % 3 <= dip)
        ]
        if not found:
            return None
        blocks = jnp.concatenate([near[g, h, place(g, h, q)] for q, _, _ in found], axis=1)
        fields = jnp.concatenate([pad[a, b] for _, a, b in found], axis=0)
        return dot(blocks, fields)

    for g, h in leaves[: len(leaves) // 2]:
        acc[g, h] = wave(g, h, (True, True))

    for j in range(1, n_col):
        part(j).wait_recv()
    total = part_send[...].astype(F32)
    for j in range(1, n_col):
        total = total + part_recv[j].astype(F32)
    tops[row] = total.astype(tops.dtype)

    def top(j, owner):
        return pltpu.make_async_remote_copy(
            src_ref=tops.at[owner], dst_ref=tops.at[owner],
            send_sem=top_sems.at[j], recv_sem=top_rsems.at[j],
            device_id={"row": lax.rem(row + j, n_row)}, device_id_type=MESH,
        )

    for j in range(1, n_row):
        top(j, row).start()
    for g, n in first_rim:
        for side in "WE":
            pl.when(has[back[side]])(lambda: rim(side, g, n).wait_recv())
    for edge in "WE":
        for side in "NS":
            pl.when(jnp.logical_and(has[side], has[edge]))(lambda: corner(side, edge).start())


    for g, h in leaves[len(leaves) // 2 :]:
        acc[g, h] = wave(g, h, (True, True))

    for j in range(1, n_row):
        top(j, lax.rem(row + n_row - j, n_row)).wait_recv()
    chosen = jnp.concatenate([tops[strips[0, a]] for a in range(n_far)], axis=0)
    c_high, c_low = split(dot(pair_high[...], chosen) + dot(pair_low[...], chosen))
    falls = dot(fall[...], jnp.concatenate([c_high, c_high, c_low], axis=0)).astype(BF16)

    for g, n in later_rim:
        for side in "WE":
            pl.when(has[back[side]])(lambda: rim(side, g, n).wait_recv())
    for g, h in leaves:
        acc[g, h] += wave(g, h, (True, False))
    for side in "NS":
        pl.when(has[back[side]])(lambda: strike(side).wait_recv())
    for g, h in leaves:
        if g in (0, along - 1):
            acc[g, h] += wave(g, h, (False, True))

    def result(g, h):
        return pltpu.make_async_copy(out.at[g, h], out_hbm.at[g, h], out_sems.at[g, h])

    def finish(g, h, value):
        k = g * dip + h
        out[g, h] = (value + dot(spread[g, h], falls[k * rank : (k + 1) * rank])).astype(out.dtype)
        result(g, h).start()

    for g, h in leaves:
        if g not in (0, along - 1):
            finish(g, h, acc[g, h])
    for g, n in first_rim + later_rim:
        for side in "WE":
            pl.when(has[side])(lambda: rim(side, g, n).wait_send())
    for side in "NS":
        pl.when(has[side])(lambda: strike(side).wait_send())
        for edge in "WE":
            pl.when(jnp.logical_and(has[side], has[edge]))(lambda: corner(side, edge).wait_send())
    for j in range(1, n_col):
        part(j).wait_send()
    for j in range(1, n_row):
        top(j, row).wait_send()
    for edge in "WE":
        for side in "NS":
            pl.when(jnp.logical_and(has[back[side]], has[edge]))(lambda: corner(side, edge).wait_recv())
    for g, h in leaves:
        if g in (0, along - 1):
            finish(g, h, acc[g, h] + wave(g, h, (False, False)))

    for g, h in leaves:
        result(g, h).wait()


def body(
    n_row,
    n_col,
    slip_rate,
    near_lists,
    near_blocks,
    source_basis,
    target_basis,
    leaf_up,
    leaf_down,
    strip_up,
    strip_down,
    strip_lists,
    coupling,
):
    along, dip, leaf, members = slip_rate.shape
    rank = source_basis.shape[2]
    n_near = near_lists.shape[2]
    n_far = coupling.shape[1]
    whole = pl.BlockSpec(memory_space=pltpu.HBM)
    dma = pltpu.SemaphoreType.DMA
    operands = [
        near_lists,
        strip_lists,
        slip_rate,
        near_blocks,
        source_basis,
        target_basis,
        leaf_up,
        leaf_down,
        strip_up,
        strip_down,
        coupling,
    ]
    pinned = [pltpu.with_memory_space_constraint(x, pltpu.HBM) for x in operands]
    return pl.pallas_call(
        functools.partial(kernel, n_row, n_col),
        out_shape=jax.ShapeDtypeStruct(slip_rate.shape, BF16),
        in_specs=[whole] * 11,
        out_specs=pl.BlockSpec(memory_space=pl.ANY),
        scratch_shapes=[
            pltpu.SMEM(near_lists.shape, jnp.int32),
            pltpu.SMEM(strip_lists.shape, jnp.int32),
            pltpu.VMEM(slip_rate.shape, BF16),
            pltpu.VMEM((along + 2, dip + 2, leaf, members), BF16),
            pltpu.VMEM((along, dip, n_near + 1, leaf, leaf), BF16),
            pltpu.VMEM(source_basis.shape, BF16),
            pltpu.VMEM(target_basis.shape, BF16),
            pltpu.VMEM(leaf_up.shape, F32),
            pltpu.VMEM(leaf_down.shape, F32),
            pltpu.VMEM(strip_up.shape, F32),
            pltpu.VMEM(strip_down.shape, F32),
            pltpu.VMEM(coupling.shape, F32),
            pltpu.VMEM(slip_rate.shape, F32),
            pltpu.VMEM((rank, members), BF16),
            pltpu.VMEM((n_col, rank, members), BF16),
            pltpu.VMEM((n_row, rank, members), BF16),
            pltpu.VMEM((along * dip * rank, 3 * rank), BF16),
            pltpu.VMEM((along, dip, leaf, rank), BF16),
            pltpu.VMEM((rank, n_far * rank), BF16),
            pltpu.VMEM((rank, n_far * rank), BF16),
            dma((11,)),
            dma((12,)),
            dma((12,)),
            dma((n_col,)),
            dma((n_col,)),
            dma((n_row,)),
            dma((n_row,)),
            dma((along, dip)),
        ],
        compiler_params=pltpu.CompilerParams(
            collective_id=0, has_side_effects=True, vmem_limit_bytes=40 * 1024 * 1024
        ),
    )(*pinned)


def solution(mesh):
    in_specs = (
        P("row", "col", None, None),
        P("row", "col", None),
        P("row", "col", None, None, None),
        P("row", "col", None, None),
        P("row", "col", None, None),
        P("row", "col", None, None),
        P("row", "col", None, None),
        P("row", None, None, None, None),
        P("row", None, None, None, None),
        P("row", None),
        P("row", None, None, None),
    )
    out_specs = P("row", "col", None, None)
    run = functools.partial(body, mesh.shape["row"], mesh.shape["col"])
    return jax.shard_map(run, mesh=mesh, in_specs=in_specs, out_specs=out_specs, check_vma=False)
```

```python
import functools

import jax
import jax.numpy as jnp
from jax import lax
from jax.experimental import pallas as pl
from jax.experimental.pallas import tpu as pltpu
from jax.sharding import PartitionSpec as P

F32, BF16 = jnp.float32, jnp.bfloat16
MESH = pl.DeviceIdType.MESH


def dot(a, b):
    return jnp.dot(a, b, preferred_element_type=F32)


def split(x):
    high = x.astype(BF16)
    return high, (x - high.astype(F32)).astype(BF16)


def dot3(a, b):
    a_high, a_low = split(a)
    b_high, b_low = split(b)
    return dot(a_high, b_high) + (dot(a_high, b_low) + dot(a_low, b_high))


def kernel(
    n_row,
    n_col,
    lists_hbm,
    strips_hbm,
    slip_hbm,
    near_hbm,
    source_hbm,
    target_hbm,
    up_hbm,
    down_hbm,
    strip_up_hbm,
    strip_down_hbm,
    coupling_hbm,
    out_hbm,
    lists,
    strips,
    out,
    pad,
    near,
    source,
    target,
    up,
    down,
    strip_up,
    strip_down,
    coupling,
    acc,
    part_send,
    part_recv,
    tops,
    fall,
    spread,
    pair_high,
    pair_low,
    load_sem,
    halo_send,
    halo_recv,
    part_sems,
    part_rsems,
    top_sems,
    top_rsems,
    out_sems,
):
    along, dip = slip_hbm.shape[:2]
    rank = source.shape[2]
    levels = strip_up.shape[1]
    n_far = coupling.shape[1]
    n_near = lists.shape[2]
    row, col = lax.axis_index("row"), lax.axis_index("col")

    barrier = pltpu.get_barrier_semaphore()
    for j in range(1, n_row):
        pl.semaphore_signal(barrier, inc=1, device_id={"row": lax.rem(row + j, n_row)}, device_id_type=MESH)
    for j in range(1, n_col):
        pl.semaphore_signal(barrier, inc=1, device_id={"col": lax.rem(col + j, n_col)}, device_id_type=MESH)

    loads = [
        pltpu.make_async_copy(src, dst, load_sem.at[k])
        for k, (src, dst) in enumerate(
            [
                (strip_up_hbm, strip_up),
                (up_hbm, up),
                (source_hbm, source),
                (slip_hbm, pad.at[pl.ds(1, along), pl.ds(1, dip)]),
                (lists_hbm, lists),
                (strips_hbm, strips),
                (near_hbm, near.at[:, :, pl.ds(0, n_near)]),
                (coupling_hbm, coupling),
                (strip_down_hbm, strip_down),
                (down_hbm, down),
                (target_hbm, target),
            ]
        )
    ]
    for load in loads:
        load.start()

    has = {"W": col > 0, "E": col < n_col - 1, "N": row > 0, "S": row < n_row - 1}
    there = {"W": {"col": col - 1}, "E": {"col": col + 1}, "N": {"row": row - 1}, "S": {"row": row + 1}}
    back = {"W": "E", "E": "W", "N": "S", "S": "N"}
    slot_of = {}

    def halo(name, side, src, dst):
        k = slot_of.setdefault(name, len(slot_of))
        return pltpu.make_async_remote_copy(
            src_ref=src, dst_ref=dst, send_sem=halo_send.at[k], recv_sem=halo_recv.at[k],
            device_id=there[side], device_id_type=MESH,
        )

    def rim(side, g, n):
        src = slip_hbm.at[pl.ds(g, n), pl.ds(0 if side == "W" else dip - 1, 1)]
        dst = pad.at[pl.ds(1 + g, n), pl.ds(dip + 1 if side == "W" else 0, 1)]
        return halo((side, g), side, src, dst)

    def strike(side):
        src = slip_hbm.at[pl.ds(0 if side == "N" else along - 1, 1)]
        dst = pad.at[pl.ds(along + 1 if side == "N" else 0, 1), pl.ds(1, dip)]
        return halo((side, "own"), side, src, dst)

    def corner(side, edge):
        at = 0 if edge == "W" else dip + 1
        src = pad.at[pl.ds(1 if side == "N" else along, 1), pl.ds(at, 1)]
        dst = pad.at[pl.ds(along + 1 if side == "N" else 0, 1), pl.ds(at, 1)]
        return halo((side, edge), side, src, dst)

    first_rim = [(0, 1), (along - 1, 1)]
    later_rim = [(1, along - 2)]

    pl.semaphore_wait(barrier, n_row + n_col - 2)

    for g, n in first_rim:
        for side in "WE":
            pl.when(has[side])(lambda: rim(side, g, n).start())
    for side in "NS":
        pl.when(has[side])(lambda: strike(side).start())

    empty = jnp.zeros((along + 2, 1) + pad.shape[2:], pad.dtype)
    for side, at in (("W", 0), ("E", dip + 1)):
        @pl.when(jnp.logical_not(has[side]))
        def _():
            pad[:, pl.ds(at, 1)] = empty
    for side, at in (("N", 0), ("S", along + 1)):
        @pl.when(jnp.logical_not(has[side]))
        def _():
            pad[pl.ds(at, 1)] = jnp.zeros((1,) + pad.shape[1:], pad.dtype)
    near[:, :, n_near] = jnp.zeros((along, dip) + near.shape[3:], near.dtype)

    leaves = [(g, h) for g in range(along) for h in range(dip)]
    loads[0].wait()
    lift = strip_up[0, 0, lax.rem(col, 2)]
    for level in range(1, levels):
        lift = dot3(strip_up[0, level, lax.rem(col // 2**level, 2)], lift)
    loads[1].wait()
    gather_up = jnp.concatenate([up[g, h] for g, h in leaves], axis=1)
    loads[2].wait()
    loads[3].wait()
    moments = jnp.concatenate([dot(source[g, h], pad[g + 1, h + 1]) for g, h in leaves], axis=0)
    lifted = dot3(lift, dot3(gather_up, moments))
    part_send[...] = lifted.astype(part_send.dtype)

    def part(j):
        to = lax.rem(col + j, n_col)
        return pltpu.make_async_remote_copy(
            src_ref=part_send, dst_ref=part_recv.at[j],
            send_sem=part_sems.at[j], recv_sem=part_rsems.at[j],
            device_id={"col": to}, device_id_type=MESH,
        )

    for j in range(1, n_col):
        part(j).start()
    for g, n in later_rim:
        for side in "WE":
            pl.when(has[side])(lambda: rim(side, g, n).start())

    for load in loads[7:]:
        load.wait()
    pair_high[...], pair_low[...] = split(jnp.concatenate([coupling[0, a] for a in range(n_far)], axis=1))
    lower = strip_down[0, levels - 1, lax.rem(col // 2 ** (levels - 1), 2)]
    for level in reversed(range(levels - 1)):
        lower = dot3(strip_down[0, level, lax.rem(col // 2**level, 2)], lower)
    fall_high, fall_low = split(dot3(down[...].reshape(along * dip * rank, rank), lower))
    fall[...] = jnp.concatenate([fall_high, fall_low, fall_high], axis=1)
    for g, h in leaves:
        spread[g, h] = target[g, h].astype(F32).T.astype(BF16)

    for load in loads[4:7]:
        load.wait()

    def place(g, h, q):
        index = n_near
        for n in range(n_near):
            index = jnp.where(lists[g, h, n] == q, n, index)
        return index

    def wave(g, h, wanted):
        found = [
            (q, g + q // 3, h + q % 3)
            for q in range(9)
            if wanted == (1 <= g + q // 3 <= along, 1 <= h + q % 3 <= dip)
        ]
        if not found:
            return None
        blocks = jnp.concatenate([near[g, h, place(g, h, q)] for q, _, _ in found], axis=1)
        fields = jnp.concatenate([pad[a, b] for _, a, b in found], axis=0)
        return dot(blocks, fields)

    for g, h in leaves[: len(leaves) // 2]:
        acc[g, h] = wave(g, h, (True, True))

    for j in range(1, n_col):
        part(j).wait_recv()
    total = part_send[...].astype(F32)
    for j in range(1, n_col):
        total = total + part_recv[j].astype(F32)
    tops[row] = total.astype(tops.dtype)

    def top(j, owner):
        return pltpu.make_async_remote_copy(
            src_ref=tops.at[owner], dst_ref=tops.at[owner],
            send_sem=top_sems.at[j], recv_sem=top_rsems.at[j],
            device_id={"row": lax.rem(row + j, n_row)}, device_id_type=MESH,
        )

    for j in range(1, n_row):
        top(j, row).start()
    for g, n in first_rim:
        for side in "WE":
            pl.when(has[back[side]])(lambda: rim(side, g, n).wait_recv())
    for edge in "WE":
        for side in "NS":
            pl.when(jnp.logical_and(has[side], has[edge]))(lambda: corner(side, edge).start())


    for g, h in leaves[len(leaves) // 2 :]:
        acc[g, h] = wave(g, h, (True, True))

    for g, n in later_rim:
        for side in "WE":
            pl.when(has[back[side]])(lambda: rim(side, g, n).wait_recv())
    for g, h in leaves:
        acc[g, h] += wave(g, h, (True, False))
    for side in "NS":
        pl.when(has[back[side]])(lambda: strike(side).wait_recv())
    for g, h in leaves:
        if g in (0, along - 1):
            acc[g, h] += wave(g, h, (False, True))

    for j in range(1, n_row):
        top(j, lax.rem(row + n_row - j, n_row)).wait_recv()
    chosen = jnp.concatenate([tops[strips[0, a]] for a in range(n_far)], axis=0)
    c_high, c_low = split(dot(pair_high[...], chosen) + dot(pair_low[...], chosen))
    falls = dot(fall[...], jnp.concatenate([c_high, c_high, c_low], axis=0)).astype(BF16)

    def result(g, h):
        return pltpu.make_async_copy(out.at[g, h], out_hbm.at[g, h], out_sems.at[g, h])

    def finish(g, h, value):
        k = g * dip + h
        out[g, h] = (value + dot(spread[g, h], falls[k * rank : (k + 1) * rank])).astype(out.dtype)
        result(g, h).start()

    for g, h in leaves:
        if g not in (0, along - 1):
            finish(g, h, acc[g, h])
    for edge in "WE":
        for side in "NS":
            pl.when(jnp.logical_and(has[back[side]], has[edge]))(lambda: corner(side, edge).wait_recv())
    for g, h in leaves:
        if g in (0, along - 1):
            finish(g, h, acc[g, h] + wave(g, h, (False, False)))

    for g, n in first_rim + later_rim:
        for side in "WE":
            pl.when(has[side])(lambda: rim(side, g, n).wait_send())
    for side in "NS":
        pl.when(has[side])(lambda: strike(side).wait_send())
        for edge in "WE":
            pl.when(jnp.logical_and(has[side], has[edge]))(lambda: corner(side, edge).wait_send())
    for j in range(1, n_col):
        part(j).wait_send()
    for j in range(1, n_row):
        top(j, row).wait_send()
    for g, h in leaves:
        result(g, h).wait()


def body(
    n_row,
    n_col,
    slip_rate,
    near_lists,
    near_blocks,
    source_basis,
    target_basis,
    leaf_up,
    leaf_down,
    strip_up,
    strip_down,
    strip_lists,
    coupling,
):
    along, dip, leaf, members = slip_rate.shape
    rank = source_basis.shape[2]
    n_near = near_lists.shape[2]
    n_far = coupling.shape[1]
    whole = pl.BlockSpec(memory_space=pltpu.HBM)
    dma = pltpu.SemaphoreType.DMA
    operands = [
        near_lists,
        strip_lists,
        slip_rate,
        near_blocks,
        source_basis,
        target_basis,
        leaf_up,
        leaf_down,
        strip_up,
        strip_down,
        coupling,
    ]
    pinned = [pltpu.with_memory_space_constraint(x, pltpu.HBM) for x in operands]
    return pl.pallas_call(
        functools.partial(kernel, n_row, n_col),
        out_shape=jax.ShapeDtypeStruct(slip_rate.shape, BF16),
        in_specs=[whole] * 11,
        out_specs=pl.BlockSpec(memory_space=pl.ANY),
        scratch_shapes=[
            pltpu.SMEM(near_lists.shape, jnp.int32),
            pltpu.SMEM(strip_lists.shape, jnp.int32),
            pltpu.VMEM(slip_rate.shape, BF16),
            pltpu.VMEM((along + 2, dip + 2, leaf, members), BF16),
            pltpu.VMEM((along, dip, n_near + 1, leaf, leaf), BF16),
            pltpu.VMEM(source_basis.shape, BF16),
            pltpu.VMEM(target_basis.shape, BF16),
            pltpu.VMEM(leaf_up.shape, F32),
            pltpu.VMEM(leaf_down.shape, F32),
            pltpu.VMEM(strip_up.shape, F32),
            pltpu.VMEM(strip_down.shape, F32),
            pltpu.VMEM(coupling.shape, F32),
            pltpu.VMEM(slip_rate.shape, F32),
            pltpu.VMEM((rank, members), BF16),
            pltpu.VMEM((n_col, rank, members), BF16),
            pltpu.VMEM((n_row, rank, members), BF16),
            pltpu.VMEM((along * dip * rank, 3 * rank), BF16),
            pltpu.VMEM((along, dip, leaf, rank), BF16),
            pltpu.VMEM((rank, n_far * rank), BF16),
            pltpu.VMEM((rank, n_far * rank), BF16),
            dma((11,)),
            dma((12,)),
            dma((12,)),
            dma((n_col,)),
            dma((n_col,)),
            dma((n_row,)),
            dma((n_row,)),
            dma((along, dip)),
        ],
        compiler_params=pltpu.CompilerParams(
            collective_id=0, has_side_effects=True, vmem_limit_bytes=40 * 1024 * 1024
        ),
    )(*pinned)


def solution(mesh):
    in_specs = (
        P("row", "col", None, None),
        P("row", "col", None),
        P("row", "col", None, None, None),
        P("row", "col", None, None),
        P("row", "col", None, None),
        P("row", "col", None, None),
        P("row", "col", None, None),
        P("row", None, None, None, None),
        P("row", None, None, None, None),
        P("row", None),
        P("row", None, None, None),
    )
    out_specs = P("row", "col", None, None)
    run = functools.partial(body, mesh.shape["row"], mesh.shape["col"])
    return jax.shard_map(run, mesh=mesh, in_specs=in_specs, out_specs=out_specs, check_vma=False)
```

```python
import functools

import jax
import jax.numpy as jnp
from jax import lax
from jax.experimental import pallas as pl
from jax.experimental.pallas import tpu as pltpu
from jax.sharding import PartitionSpec as P

F32, BF16 = jnp.float32, jnp.bfloat16
MESH = pl.DeviceIdType.MESH


def dot(a, b):
    return jnp.dot(a, b, preferred_element_type=F32)


def split(x):
    high = x.astype(BF16)
    return high, (x - high.astype(F32)).astype(BF16)


def dot3(a, b):
    a_high, a_low = split(a)
    b_high, b_low = split(b)
    return dot(a_high, b_high) + (dot(a_high, b_low) + dot(a_low, b_high))


def kernel(
    n_row,
    n_col,
    lists_hbm,
    strips_hbm,
    slip_hbm,
    near_hbm,
    source_hbm,
    target_hbm,
    up_hbm,
    down_hbm,
    strip_up_hbm,
    strip_down_hbm,
    coupling_hbm,
    out_hbm,
    lists,
    strips,
    out,
    pad,
    near,
    source,
    target,
    up,
    down,
    strip_up,
    strip_down,
    coupling,
    acc,
    part_send,
    part_recv,
    tops,
    fall,
    spread,
    pair_high,
    pair_low,
    load_sem,
    halo_send,
    halo_recv,
    part_sems,
    part_rsems,
    top_sems,
    top_rsems,
    out_sems,
):
    along, dip = slip_hbm.shape[:2]
    rank = source.shape[2]
    levels = strip_up.shape[1]
    n_far = coupling.shape[1]
    n_near = lists.shape[2]
    row, col = lax.axis_index("row"), lax.axis_index("col")

    barrier = pltpu.get_barrier_semaphore()
    for j in range(1, n_row):
        pl.semaphore_signal(barrier, inc=1, device_id={"row": lax.rem(row + j, n_row)}, device_id_type=MESH)
    for j in range(1, n_col):
        pl.semaphore_signal(barrier, inc=1, device_id={"col": lax.rem(col + j, n_col)}, device_id_type=MESH)

    loads = [
        pltpu.make_async_copy(src, dst, load_sem.at[k])
        for k, (src, dst) in enumerate(
            [
                (strip_up_hbm, strip_up),
                (up_hbm, up),
                (source_hbm, source),
                (slip_hbm, pad.at[pl.ds(1, along), pl.ds(1, dip)]),
                (lists_hbm, lists),
                (strips_hbm, strips),
                (near_hbm, near.at[:, :, pl.ds(0, n_near)]),
                (coupling_hbm, coupling),
                (strip_down_hbm, strip_down),
                (down_hbm, down),
                (target_hbm, target),
            ]
        )
    ]
    for load in loads:
        load.start()

    has = {"W": col > 0, "E": col < n_col - 1, "N": row > 0, "S": row < n_row - 1}
    there = {"W": {"col": col - 1}, "E": {"col": col + 1}, "N": {"row": row - 1}, "S": {"row": row + 1}}
    back = {"W": "E", "E": "W", "N": "S", "S": "N"}
    slot_of = {}

    def halo(name, side, src, dst):
        k = slot_of.setdefault(name, len(slot_of))
        return pltpu.make_async_remote_copy(
            src_ref=src, dst_ref=dst, send_sem=halo_send.at[k], recv_sem=halo_recv.at[k],
            device_id=there[side], device_id_type=MESH,
        )

    def rim(side, g, n):
        src = slip_hbm.at[pl.ds(g, n), pl.ds(0 if side == "W" else dip - 1, 1)]
        dst = pad.at[pl.ds(1 + g, n), pl.ds(dip + 1 if side == "W" else 0, 1)]
        return halo((side, g), side, src, dst)

    def strike(side):
        src = slip_hbm.at[pl.ds(0 if side == "N" else along - 1, 1)]
        dst = pad.at[pl.ds(along + 1 if side == "N" else 0, 1), pl.ds(1, dip)]
        return halo((side, "own"), side, src, dst)

    def corner(side, edge):
        at = 0 if edge == "W" else dip + 1
        src = pad.at[pl.ds(1 if side == "N" else along, 1), pl.ds(at, 1)]
        dst = pad.at[pl.ds(along + 1 if side == "N" else 0, 1), pl.ds(at, 1)]
        return halo((side, edge), side, src, dst)

    first_rim = [(0, 1), (along - 1, 1)]
    later_rim = [(1, along - 2)]

    empty = jnp.zeros((along + 2, 1) + pad.shape[2:], pad.dtype)
    for side, at in (("W", 0), ("E", dip + 1)):
        @pl.when(jnp.logical_not(has[side]))
        def _():
            pad[:, pl.ds(at, 1)] = empty
    for side, at in (("N", 0), ("S", along + 1)):
        @pl.when(jnp.logical_not(has[side]))
        def _():
            pad[pl.ds(at, 1)] = jnp.zeros((1,) + pad.shape[1:], pad.dtype)
    near[:, :, n_near] = jnp.zeros((along, dip) + near.shape[3:], near.dtype)

    leaves = [(g, h) for g in range(along) for h in range(dip)]
    loads[0].wait()
    lift = strip_up[0, 0, lax.rem(col, 2)]
    for level in range(1, levels):
        lift = dot3(strip_up[0, level, lax.rem(col // 2**level, 2)], lift)
    loads[1].wait()
    gather_up = jnp.concatenate([up[g, h] for g, h in leaves], axis=1)
    loads[2].wait()
    loads[3].wait()
    moments = jnp.concatenate([dot(source[g, h], pad[g + 1, h + 1]) for g, h in leaves], axis=0)
    lifted = dot3(lift, dot3(gather_up, moments))
    part_send[...] = lifted.astype(part_send.dtype)

    def part(j):
        to = lax.rem(col + j, n_col)
        return pltpu.make_async_remote_copy(
            src_ref=part_send, dst_ref=part_recv.at[j],
            send_sem=part_sems.at[j], recv_sem=part_rsems.at[j],
            device_id={"col": to}, device_id_type=MESH,
        )

    pl.semaphore_wait(barrier, n_row + n_col - 2)

    for j in range(1, n_col):
        part(j).start()
    for g, n in first_rim:
        for side in "WE":
            pl.when(has[side])(lambda: rim(side, g, n).start())
    for side in "NS":
        pl.when(has[side])(lambda: strike(side).start())
    for g, n in later_rim:
        for side in "WE":
            pl.when(has[side])(lambda: rim(side, g, n).start())

    for load in loads[7:]:
        load.wait()
    pair_high[...], pair_low[...] = split(jnp.concatenate([coupling[0, a] for a in range(n_far)], axis=1))
    lower = strip_down[0, levels - 1, lax.rem(col // 2 ** (levels - 1), 2)]
    for level in reversed(range(levels - 1)):
        lower = dot3(strip_down[0, level, lax.rem(col // 2**level, 2)], lower)
    fall_high, fall_low = split(dot3(down[...].reshape(along * dip * rank, rank), lower))
    fall[...] = jnp.concatenate([fall_high, fall_low, fall_high], axis=1)
    for g, h in leaves:
        spread[g, h] = target[g, h].astype(F32).T.astype(BF16)

    for load in loads[4:7]:
        load.wait()

    def place(g, h, q):
        index = n_near
        for n in range(n_near):
            index = jnp.where(lists[g, h, n] == q, n, index)
        return index

    def wave(g, h, wanted):
        found = [
            (q, g + q // 3, h + q % 3)
            for q in range(9)
            if wanted == (1 <= g + q // 3 <= along, 1 <= h + q % 3 <= dip)
        ]
        if not found:
            return None
        blocks = jnp.concatenate([near[g, h, place(g, h, q)] for q, _, _ in found], axis=1)
        fields = jnp.concatenate([pad[a, b] for _, a, b in found], axis=0)
        return dot(blocks, fields)

    for g, h in leaves[: len(leaves) // 2]:
        acc[g, h] = wave(g, h, (True, True))

    for j in range(1, n_col):
        part(j).wait_recv()
    total = part_send[...].astype(F32)
    for j in range(1, n_col):
        total = total + part_recv[j].astype(F32)
    tops[row] = total.astype(tops.dtype)

    def top(j, owner):
        return pltpu.make_async_remote_copy(
            src_ref=tops.at[owner], dst_ref=tops.at[owner],
            send_sem=top_sems.at[j], recv_sem=top_rsems.at[j],
            device_id={"row": lax.rem(row + j, n_row)}, device_id_type=MESH,
        )

    for j in range(1, n_row):
        top(j, row).start()
    for g, n in first_rim:
        for side in "WE":
            pl.when(has[back[side]])(lambda: rim(side, g, n).wait_recv())
    for edge in "WE":
        for side in "NS":
            pl.when(jnp.logical_and(has[side], has[edge]))(lambda: corner(side, edge).start())


    for g, h in leaves[len(leaves) // 2 :]:
        acc[g, h] = wave(g, h, (True, True))

    for g, n in later_rim:
        for side in "WE":
            pl.when(has[back[side]])(lambda: rim(side, g, n).wait_recv())
    for g, h in leaves:
        acc[g, h] += wave(g, h, (True, False))
    for side in "NS":
        pl.when(has[back[side]])(lambda: strike(side).wait_recv())
    for g, h in leaves:
        if g in (0, along - 1):
            acc[g, h] += wave(g, h, (False, True))

    for j in range(1, n_row):
        top(j, lax.rem(row + n_row - j, n_row)).wait_recv()
    chosen = jnp.concatenate([tops[strips[0, a]] for a in range(n_far)], axis=0)
    c_high, c_low = split(dot(pair_high[...], chosen) + dot(pair_low[...], chosen))
    falls = dot(fall[...], jnp.concatenate([c_high, c_high, c_low], axis=0)).astype(BF16)

    def result(g, h):
        return pltpu.make_async_copy(out.at[g, h], out_hbm.at[g, h], out_sems.at[g, h])

    def finish(g, h, value):
        k = g * dip + h
        out[g, h] = (value + dot(spread[g, h], falls[k * rank : (k + 1) * rank])).astype(out.dtype)
        result(g, h).start()

    for g, h in leaves:
        if g not in (0, along - 1):
            finish(g, h, acc[g, h])
    for edge in "WE":
        for side in "NS":
            pl.when(jnp.logical_and(has[back[side]], has[edge]))(lambda: corner(side, edge).wait_recv())
    for g, h in leaves:
        if g in (0, along - 1):
            finish(g, h, acc[g, h] + wave(g, h, (False, False)))

    for g, n in first_rim + later_rim:
        for side in "WE":
            pl.when(has[side])(lambda: rim(side, g, n).wait_send())
    for side in "NS":
        pl.when(has[side])(lambda: strike(side).wait_send())
        for edge in "WE":
            pl.when(jnp.logical_and(has[side], has[edge]))(lambda: corner(side, edge).wait_send())
    for j in range(1, n_col):
        part(j).wait_send()
    for j in range(1, n_row):
        top(j, row).wait_send()
    for g, h in leaves:
        result(g, h).wait()


def body(
    n_row,
    n_col,
    slip_rate,
    near_lists,
    near_blocks,
    source_basis,
    target_basis,
    leaf_up,
    leaf_down,
    strip_up,
    strip_down,
    strip_lists,
    coupling,
):
    along, dip, leaf, members = slip_rate.shape
    rank = source_basis.shape[2]
    n_near = near_lists.shape[2]
    n_far = coupling.shape[1]
    whole = pl.BlockSpec(memory_space=pltpu.HBM)
    dma = pltpu.SemaphoreType.DMA
    operands = [
        near_lists,
        strip_lists,
        slip_rate,
        near_blocks,
        source_basis,
        target_basis,
        leaf_up,
        leaf_down,
        strip_up,
        strip_down,
        coupling,
    ]
    pinned = [pltpu.with_memory_space_constraint(x, pltpu.HBM) for x in operands]
    return pl.pallas_call(
        functools.partial(kernel, n_row, n_col),
        out_shape=jax.ShapeDtypeStruct(slip_rate.shape, BF16),
        in_specs=[whole] * 11,
        out_specs=pl.BlockSpec(memory_space=pl.ANY),
        scratch_shapes=[
            pltpu.SMEM(near_lists.shape, jnp.int32),
            pltpu.SMEM(strip_lists.shape, jnp.int32),
            pltpu.VMEM(slip_rate.shape, BF16),
            pltpu.VMEM((along + 2, dip + 2, leaf, members), BF16),
            pltpu.VMEM((along, dip, n_near + 1, leaf, leaf), BF16),
            pltpu.VMEM(source_basis.shape, BF16),
            pltpu.VMEM(target_basis.shape, BF16),
            pltpu.VMEM(leaf_up.shape, F32),
            pltpu.VMEM(leaf_down.shape, F32),
            pltpu.VMEM(strip_up.shape, F32),
            pltpu.VMEM(strip_down.shape, F32),
            pltpu.VMEM(coupling.shape, F32),
            pltpu.VMEM(slip_rate.shape, F32),
            pltpu.VMEM((rank, members), BF16),
            pltpu.VMEM((n_col, rank, members), BF16),
            pltpu.VMEM((n_row, rank, members), BF16),
            pltpu.VMEM((along * dip * rank, 3 * rank), BF16),
            pltpu.VMEM((along, dip, leaf, rank), BF16),
            pltpu.VMEM((rank, n_far * rank), BF16),
            pltpu.VMEM((rank, n_far * rank), BF16),
            dma((11,)),
            dma((12,)),
            dma((12,)),
            dma((n_col,)),
            dma((n_col,)),
            dma((n_row,)),
            dma((n_row,)),
            dma((along, dip)),
        ],
        compiler_params=pltpu.CompilerParams(
            collective_id=0, has_side_effects=True, vmem_limit_bytes=40 * 1024 * 1024
        ),
    )(*pinned)


def solution(mesh):
    in_specs = (
        P("row", "col", None, None),
        P("row", "col", None),
        P("row", "col", None, None, None),
        P("row", "col", None, None),
        P("row", "col", None, None),
        P("row", "col", None, None),
        P("row", "col", None, None),
        P("row", None, None, None, None),
        P("row", None, None, None, None),
        P("row", None),
        P("row", None, None, None),
    )
    out_specs = P("row", "col", None, None)
    run = functools.partial(body, mesh.shape["row"], mesh.shape["col"])
    return jax.shard_map(run, mesh=mesh, in_specs=in_specs, out_specs=out_specs, check_vma=False)
```
